32 devices in a mesh: groups: 2 (over x), tm: 2 (over core), space: 8 (over z, y).
Axes of the slice: x: 2, y: 2, z: 4, core: 2. Of those that a mesh axis runs over, the one named last changes fastest.
Arguments:
- nodes: float32 [4, 3, 32, 256, 256], P(('groups', 'tm'), None, 'space'), parts along dimension 0, may hold values from -1 to 1
Outputs:
- updated: float32 [4, 3, 32, 256, 256], P(('groups', 'tm'), None, 'space'), parts along dimension 0
The draws below stay inside these ranges and needn't reach their ends.
There are 2 independent parts, one for each index of `groups`. The reference program is written for one: setup_inputs(seed, part) draws one part's arguments, and reference() takes and returns one part's arrays. A program takes and returns all parts, laid end to end along the dimension named above; each array names one. Nothing has to cross between parts.
All inputs are finite; a program needn't handle non-finite values.
Results may differ from the reference program's by a relative error of at most 0.0001.
Values sent between devices are 32-bit elements; how exact they have to be, the bound alone decides.
No kernel may reach another device: no remote copies, remote signals or barrier semaphores. Data moves between devices by JAX's collectives and lax.ppermute only.
A program may use at most 448 MiB of HBM per device.

```python
import jax
import jax.numpy as jnp

NY = 256
NZ = 256
NX = 32
SECTIONS = 2


def block_levels(key, dims, pieces, low, top_value):
    loudness, own = 1.0, jax.random.fold_in(key, 6)
    for dim, parts in pieces:
        steps = jnp.exp(jax.random.uniform(jax.random.fold_in(own, dim), (parts,), jnp.float32, low / len(pieces), top_value / len(pieces)))
        loudness = loudness * jnp.repeat(steps, dims[dim] // parts).reshape([-1 if axis == dim else 1 for axis in range(len(dims))])
    return loudness


def setup_inputs(seed: int = 0, part: int = 0) -> dict:
    key_list = jax.random.split(jax.random.key(seed), 2)
    part_splits = jax.random.split(jax.random.fold_in(key_list[1], part), 2)
    nodes = jnp.clip(jax.random.uniform(part_splits[0], (SECTIONS, 3, NX, NY, NZ), jnp.float32, -1.0, 1.0) * block_levels(part_splits[0], (SECTIONS, 3, NX, NY, NZ), ((0, 2), (2, 8)), -0.4, 0.0), -1.0, 1.0)
    return dict(nodes=nodes)


DIFFUSE = 0.12
GROWTH = 0.5
WEIGHTS = ((5.0 / 24.0, 1.0 / 3.0, -1.0 / 24.0), (-1.0 / 24.0, 1.0 / 3.0, 5.0 / 24.0))


def laplace_force(field, coeff):
    laplace = jnp.roll(field, 1, -3) + jnp.roll(field, -1, -3)
    laplace = laplace + jnp.roll(field, 1, -2) + jnp.roll(field, -1, -2)
    laplace = laplace + jnp.roll(field, 1, -1) + jnp.roll(field, -1, -1) - 6.0 * field
    return coeff * laplace + GROWTH * (field - field * field * field)


def quadrature(row, stacked):
    return WEIGHTS[row][0] * stacked[0] + WEIGHTS[row][1] * stacked[1] + WEIGHTS[row][2] * stacked[2]


def restrict(field):
    shape = field.shape
    blocks = field.reshape(shape[:-3] + (shape[-3] // 2, 2, shape[-2] // 2, 2, shape[-1] // 2, 2))
    return jnp.mean(blocks, axis=(-5, -3, -1))


def prolong(field):
    for axis_at in (-3, -2, -1):
        field = jnp.repeat(field, 2, axis=axis_at)
    return field


def reference(nodes):
    coarse_coeff = DIFFUSE / 4.0
    results = []
    carried_fine = None
    carried_coarse = None
    for section in range(SECTIONS):
        current = nodes[section]
        forces = laplace_force(current, DIFFUSE)
        node_one = current[0] + quadrature(0, forces)
        force_one = laplace_force(node_one, DIFFUSE)
        node_two = node_one + 0.5 * (force_one - forces[1]) + quadrature(1, forces)
        force_two = laplace_force(node_two, DIFFUSE)
        start = current[0] if section == 0 else carried_fine
        coarse_nodes = restrict(jnp.stack([current[0], node_one, node_two]))
        coarse_forces = laplace_force(coarse_nodes, coarse_coeff)
        difference = restrict(jnp.stack([forces[0], force_one, force_two])) - coarse_forces
        coarse_start = restrict(start)
        first = coarse_start if section == 0 else carried_coarse
        coarse_one = first + 0.5 * (laplace_force(first, coarse_coeff) - coarse_forces[0]) + quadrature(0, coarse_forces) + quadrature(0, difference)
        coarse_two = coarse_one + 0.5 * (laplace_force(coarse_one, coarse_coeff) - coarse_forces[1]) + quadrature(1, coarse_forces) + quadrature(1, difference)
        new_zero = start + prolong(first - coarse_start)
        new_one = node_one + prolong(coarse_one - coarse_nodes[1])
        new_two = node_two + prolong(coarse_two - coarse_nodes[2])
        results.append(jnp.stack([new_zero, new_one, new_two]))
        carried_fine = node_two
        carried_coarse = coarse_two
    return jnp.stack(results)
```

```python
import jax
import jax.numpy as jnp
from jax import lax
from jax.experimental import pallas as pl
from jax.experimental.pallas import tpu as pltpu
from jax.sharding import PartitionSpec as P

DIFFUSE = 0.12
COARSE = DIFFUSE / 4.0
GROWTH = 0.5
WEIGHTS = ((5.0 / 24.0, 1.0 / 3.0, -1.0 / 24.0), (-1.0 / 24.0, 1.0 / 3.0, 5.0 / 24.0))
SECOND = (WEIGHTS[1][0], WEIGHTS[1][1] - 0.5, WEIGHTS[1][2])
LANES = 128
F32 = jnp.float32
BF16 = jnp.bfloat16
VMEM_LIMIT = 32 * 1024 * 1024


def combine(weights, parts):
    return weights[0] * parts[0] + weights[1] * parts[1] + weights[2] * parts[2]


def cube(v):
    return v * v * v


def z_neighbours(halves):
    count = len(halves)
    lane = lax.broadcasted_iota(jnp.int32, halves[0].shape, 1)
    fwd = [pltpu.roll(v, 1, 1) for v in halves]
    back = [pltpu.roll(v, LANES - 1, 1) for v in halves]
    out = []
    for k in range(count):
        before = jnp.where(lane == 0, fwd[(k - 1) % count], fwd[k])
        after = jnp.where(lane == LANES - 1, back[(k + 1) % count], back[k])
        out.append(before + after)
    return out


def y_neighbours(other, parity):
    rows = other.shape[0]
    return other + pltpu.roll(other, 1 if parity == 0 else rows - 1, 0)


def laplace_planes(ref, plane, planes, halves):
    for parity in range(2):
        own = [ref[plane, h, parity] for h in range(halves)]
        side = z_neighbours(own)
        for h in range(halves):
            total = side[h] + y_neighbours(ref[plane, h, 1 - parity], parity) - 6.0 * own[h]
            if plane > 0:
                total = total + ref[plane - 1, h, parity]
            if plane < planes - 1:
                total = total + ref[plane + 1, h, parity]
            yield h, parity, own[h], total


def coarse_force(field):
    planes = len(field)
    out = []
    for p in range(planes):
        v = field[p]
        rows, lanes = v.shape
        total = pltpu.roll(v, 1, 0) + pltpu.roll(v, rows - 1, 0)
        total = total + pltpu.roll(v, 1, 1) + pltpu.roll(v, lanes - 1, 1) - 6.0 * v
        if p > 0:
            total = total + field[p - 1]
        if p < planes - 1:
            total = total + field[p + 1]
        out.append(COARSE * total + GROWTH * (v - cube(v)))
    return out


def split(v):
    high = v.astype(BF16)
    low = (v - high.astype(F32)).astype(BF16)
    return high, low


def pair_matrix(size):
    row = lax.broadcasted_iota(jnp.int32, (size, size // 2), 0)
    col = lax.broadcasted_iota(jnp.int32, (size, size // 2), 1)
    offset = lax.rem(row - 2 * col + size, size)
    inner = offset < 2
    outer = (offset == 2) | (offset == size - 1)
    sums = jnp.where(inner, 1.0, 0.0).astype(F32)
    bends = jnp.where(outer, 1.0, 0.0).astype(F32) - sums
    return sums.astype(BF16), bends.astype(BF16)


def spread_matrix(size):
    row = lax.broadcasted_iota(jnp.int32, (size, 2 * size), 0)
    col = lax.broadcasted_iota(jnp.int32, (size, 2 * size), 1)
    return jnp.where((col == 2 * row) | (col == 2 * row + 1), 1.0, 0.0).astype(F32).astype(BF16)


def times(v, matrix):
    high, low = split(v)
    return jnp.dot(high, matrix, preferred_element_type=F32) + jnp.dot(
        low, matrix, preferred_element_type=F32
    )


def restrict_field(ref, planes, halves):
    size = halves * LANES
    sums, bends = pair_matrix(size)

    def y_sum(p):
        return [ref[p, h, 0] + ref[p, h, 1] for h in range(halves)]

    means, forces = [], []
    flat = [y_sum(p) for p in range(planes)]
    for top in range(0, planes, 2):
        total, rest = [], []
        for h in range(halves):
            even = ref[top, h, 0] + ref[top + 1, h, 0]
            odd = ref[top, h, 1] + ref[top + 1, h, 1]
            both = even + odd
            rows = both.shape[0]
            flux = pltpu.roll(odd, 1, 0) + pltpu.roll(even, rows - 1, 0) - 2.0 * both
            if top > 0:
                flux = flux + flat[top - 1][h]
            if top + 2 < planes:
                flux = flux + flat[top + 2][h]
            cubes = cube(ref[top, h, 0]) + cube(ref[top + 1, h, 0])
            cubes = cubes + cube(ref[top, h, 1]) + cube(ref[top + 1, h, 1])
            total.append(both)
            rest.append(DIFFUSE * flux + GROWTH * (both - cubes))
        total = jnp.concatenate(total, axis=1)
        rest = jnp.concatenate(rest, axis=1)
        means.append(times(total, sums) * 0.125)
        forces.append((times(rest, sums) + DIFFUSE * times(total, bends)) * 0.125)
    edges = [times(jnp.concatenate(flat[p], axis=1), sums) for p in (0, planes - 1)]
    return means, forces, edges


def store_coarse(out, means, forces, edges):
    for k, parts in enumerate((means, forces, edges)):
        for p, v in enumerate(parts):
            out[k, p] = v


def edge_kernel(nodes, first, last, held, sem):
    planes, halves = nodes.shape[2], held.shape[2]
    copies = []
    for e, p in enumerate((0, planes - 1)):
        for m in range(3):
            for h in range(halves):
                copies.append(
                    pltpu.make_async_copy(
                        nodes.at[0, m, p, :, pl.ds(h * LANES, LANES)],
                        held.at[e, m, h],
                        sem.at[e, m, h],
                    )
                )
    for copy in copies:
        copy.start()
    for copy in copies:
        copy.wait()
    rows = first.shape[2]
    for e, out in enumerate((first, last)):
        for h in range(halves):
            for q in range(2):
                parts = [held[e, m, h, pl.ds(q, rows, stride=2), :] for m in range(3)]
                out[h, q] = combine(WEIGHTS[0], parts)


def first_kernel(nodes, one, slope, rest, edge_low, edge_high, coarse, held, start, mix, sem):
    planes, halves = nodes.shape[2], held.shape[2]
    rows = one.shape[3]
    copies = [
        [
            pltpu.make_async_copy(
                nodes.at[0, m, p, :, pl.ds(h * LANES, LANES)], held.at[m, p, h], sem.at[m, p, h]
            )
            for m in range(3)
            for h in range(halves)
        ]
        for p in range(planes)
    ]
    for group in copies:
        for copy in group:
            copy.start()
    for p in range(planes):
        for copy in copies[p]:
            copy.wait()
        for h in range(halves):
            for q in range(2):
                parts = [held[m, p, h, pl.ds(q, rows, stride=2), :] for m in range(3)]
                cubes = [cube(v) for v in parts]
                a = combine(WEIGHTS[0], parts)
                d = combine(SECOND, parts)
                start[p, h, q] = parts[0]
                mix[p, h, q] = a
                slope[p, h, q] = d
                one[p, h, q] = parts[0] + GROWTH * (a - combine(WEIGHTS[0], cubes))
                rest[p, h, q] = GROWTH * (d - combine(SECOND, cubes))
    for p in range(planes):
        for h, q, _, laplace in laplace_planes(mix, p, planes, halves):
            value = one[p, h, q] + DIFFUSE * laplace
            one[p, h, q] = value
            if p == 0:
                edge_low[h, q] = 0.5 * value + slope[p, h, q]
            if p == planes - 1:
                edge_high[h, q] = 0.5 * value + slope[p, h, q]
    store_coarse(coarse, *restrict_field(start, planes, halves))


def second_kernel(one_in, slope, rest, low, high, own_low, own_high, one, two, coarse, mix):
    planes, halves = one_in.shape[0], one_in.shape[1]
    for p in range(planes):
        for h in range(halves):
            for q in range(2):
                value = one_in[p, h, q]
                if p == 0:
                    value = value + DIFFUSE * low[h, q]
                if p == planes - 1:
                    value = value + DIFFUSE * high[h, q]
                one[p, h, q] = value
                mix[p, h, q] = 0.5 * value + slope[p, h, q]
    for p in range(planes):
        for h, q, _, laplace in laplace_planes(mix, p, planes, halves):
            if p == 0:
                laplace = laplace + (0.5 * DIFFUSE) * own_low[h, q]
            if p == planes - 1:
                laplace = laplace + (0.5 * DIFFUSE) * own_high[h, q]
            value = one[p, h, q]
            two[p, h, q] = (
                value + DIFFUSE * laplace + (0.5 * GROWTH) * (value - cube(value)) + rest[p, h, q]
            )
    store_coarse(coarse, *restrict_field(one, planes, halves))


def third_kernel(two_in, low, high, coarse_zero, coarse_one, two, send_low, send_high, work):
    planes, halves = two_in.shape[0], two_in.shape[1]
    later = lax.axis_index("tm").astype(F32)
    for p in range(planes):
        for h in range(halves):
            for q in range(2):
                value = two_in[p, h, q]
                if p == 0:
                    value = value + DIFFUSE * low[h, q]
                if p == planes - 1:
                    value = value + DIFFUSE * high[h, q]
                two[p, h, q] = value
    means_two, forces_two, edges_two = restrict_field(two, planes, halves)
    half = planes // 2
    zero = [coarse_zero[0, p] for p in range(half)]
    mean_one = [coarse_one[0, p] for p in range(half)]
    force_zero = coarse_force(zero)
    force_one = coarse_force(mean_one)
    sweep_zero, sweep_one = [], []
    for p in range(half):
        parts = (coarse_zero[1, p], coarse_one[1, p], forces_two[p])
        sweep_zero.append(combine(WEIGHTS[0], parts))
        sweep_one.append(combine(WEIGHTS[1], parts))
    for e, (p, out) in enumerate(((0, send_low), (half - 1, send_high))):
        parts = (coarse_zero[2, e], coarse_one[2, e], edges_two[e])
        partial = sweep_zero[p] - mean_one[p] + (1.0 - later) * zero[p] - (0.5 * later) * force_zero[p]
        out[0] = (DIFFUSE / 8.0) * combine(WEIGHTS[0], parts) - (0.5 * COARSE * later) * zero[p]
        out[1] = (DIFFUSE / 8.0) * combine(WEIGHTS[1], parts) + (0.5 * COARSE) * partial
    for p in range(half):
        work[0, p] = zero[p]
        work[1, p] = mean_one[p]
        work[2, p] = means_two[p]
        work[3, p] = sweep_zero[p] - 0.5 * force_zero[p]
        work[4, p] = sweep_one[p] - 0.5 * force_one[p]


def coarse_chain(first, first_low, first_high, bend_low, bend_high, work, low, high, own_low, own_high):
    half = len(first)
    force = coarse_force(first)
    one = []
    for p in range(half):
        v = first[p] + 0.5 * force[p] + work[3, p]
        if p == 0:
            v = v + low[0] + first_low
        if p == half - 1:
            v = v + high[0] + first_high
        one.append(v)
    force = coarse_force(one)
    two = []
    for p in range(half):
        v = one[p] + 0.5 * force[p] + work[4, p]
        if p == 0:
            v = v + low[1] + (0.5 * COARSE) * (own_low[0] + bend_low)
        if p == half - 1:
            v = v + high[1] + (0.5 * COARSE) * (own_high[0] + bend_high)
        two.append(v)
    return one, two


def fourth_kernel(work, low, high, own_low, own_high, partner, send_low, send_high):
    half = work.shape[1]
    first = [work[0, p] for p in range(half)]
    one, two = coarse_chain(first, 0.0, 0.0, 0.0, 0.0, work, low, high, own_low, own_high)
    force = coarse_force(two)
    for p in range(half):
        partner[0, p] = two[p]
        partner[1, p] = two[p] - work[2, p]
    for p, out in ((0, send_low), (half - 1, send_high)):
        out[0] = two[p]
        out[1] = two[p] + 0.5 * force[p]


def last_kernel(
    nodes, one, two, moved, work, low, high, own_low, own_high, partner, ring_low, ring_high,
    updated, held, result, load_sem, store_sem,
):
    planes, halves = one.shape[0], one.shape[1]
    rows = one.shape[3]
    half = planes // 2
    section = lax.axis_index("tm")
    later = section.astype(F32)
    loads = [
        pltpu.make_async_copy(
            nodes.at[0, 0, :, :, pl.ds(h * LANES, LANES)], held.at[:, h], load_sem.at[h]
        )
        for h in range(halves)
    ]
    for copy in loads:
        copy.start()
    first, change = [], []
    for p in range(half):
        first.append(jnp.where(section == 0, work[0, p], partner[0, p]))
        change.append(jnp.where(section == 0, first[p] - work[0, p], partner[1, p]))
    scale = 0.5 * COARSE
    coarse_one, coarse_two = coarse_chain(
        first,
        (scale * later) * ring_low[0],
        (scale * later) * ring_high[0],
        later * (ring_low[1] + scale * first[0]),
        later * (ring_high[1] + scale * first[half - 1]),
        work, low, high, own_low, own_high,
    )
    spread = spread_matrix(LANES * halves // 2)
    stores = []

    def put(node, p):
        for h in range(halves):
            copy = pltpu.make_async_copy(
                result.at[node, p, h],
                updated.at[0, node, p, :, pl.ds(h * LANES, LANES)],
                store_sem.at[node, p, h],
            )
            copy.start()
            stores.append(copy)

    for node, base in ((1, one), (2, two)):
        for top in range(half):
            diff = (coarse_one[top] if node == 1 else coarse_two[top]) - work[node, top]
            wide = times(diff, spread)
            for p in (2 * top, 2 * top + 1):
                for h in range(halves):
                    for q in range(2):
                        result[node, p, h, pl.ds(q, rows, stride=2), :] = (
                            base[p, h, q] + wide[:, h * LANES : (h + 1) * LANES]
                        )
                put(node, p)
    for copy in loads:
        copy.wait()
    for top in range(half):
        wide = times(change[top], spread)
        for p in (2 * top, 2 * top + 1):
            for h in range(halves):
                for q in range(2):
                    own = held[p, h, pl.ds(q, rows, stride=2), :]
                    start = jnp.where(section == 0, own, moved[p, h, q])
                    result[0, p, h, pl.ds(q, rows, stride=2), :] = (
                        start + wide[:, h * LANES : (h + 1) * LANES]
                    )
            put(0, p)
    for copy in stores:
        copy.wait()


def call(kernel, name, inputs, any_inputs, outs, scratch=(), any_out=False, flops=0, size=0):
    vmem = pl.BlockSpec(memory_space=pltpu.VMEM)
    hbm = pl.BlockSpec(memory_space=pl.ANY)
    return pl.pallas_call(
        kernel,
        name=name,
        out_shape=[jax.ShapeDtypeStruct(s, F32) for s in outs],
        in_specs=[hbm if k < any_inputs else vmem for k in range(len(inputs))],
        out_specs=[hbm if any_out else vmem for _ in outs],
        scratch_shapes=list(scratch),
        compiler_params=pltpu.CompilerParams(vmem_limit_bytes=VMEM_LIMIT),
        cost_estimate=pl.CostEstimate(flops=flops, bytes_accessed=size, transcendentals=0),
    )(*inputs)


def exchange(low, high, axis):
    peers = lax.axis_size(axis)
    up = [(i, (i + 1) % peers) for i in range(peers)]
    down = [(j, i) for i, j in up]
    return lax.ppermute(high, axis, up), lax.ppermute(low, axis, down)


def local(nodes):
    _, _, planes, ny, nz = nodes.shape
    halves, rows, half = nz // LANES, ny // 2, planes // 2
    plane = (halves, 2, rows, LANES)
    field = (planes,) + plane
    quarter = (rows, nz // 2)
    pair = (2,) + quarter
    packed = (3, half) + quarter
    size = planes * ny * nz * 4

    a_low, a_high = call(
        edge_kernel, "edge_mix", (nodes,), 1, [plane, plane],
        [pltpu.VMEM((2, 3, halves, ny, LANES), F32), pltpu.SemaphoreType.DMA((2, 3, halves))],
        size=size * 2, flops=size,
    )
    a_below, a_above = exchange(a_low, a_high, "space")
    one_part, slope, rest, b_low, b_high, coarse_zero = call(
        first_kernel, "first_stage", (nodes,), 1, [field, field, field, plane, plane, packed],
        [
            pltpu.VMEM((3, planes, halves, ny, LANES), F32),
            pltpu.VMEM(field, F32),
            pltpu.VMEM(field, F32),
            pltpu.SemaphoreType.DMA((3, planes, halves)),
        ],
        size=size * 6, flops=size * 10,
    )
    b_below, b_above = exchange(b_low, b_high, "space")
    one, two_part, coarse_mid = call(
        second_kernel, "second_stage",
        (one_part, slope, rest, a_below, a_above, a_low, a_high), 0,
        [field, field, packed], [pltpu.VMEM(field, F32)],
        size=size * 6, flops=size * 10,
    )
    two, h_low, h_high, work = call(
        third_kernel, "third_stage", (two_part, b_below, b_above, coarse_zero, coarse_mid), 0,
        [field, pair, pair, (5, half) + quarter],
        size=size * 3, flops=size * 5,
    )
    below, above = exchange(h_low, h_high, "space")
    moved = lax.ppermute(two, "tm", [(0, 1)])
    partner, f_low, f_high = call(
        fourth_kernel, "coarse_chain", (work, below, above, h_low, h_high), 0,
        [(2, half) + quarter, pair, pair],
        size=size, flops=size,
    )
    peers = lax.axis_size("space")
    to_above = [(i, peers + (i + 1) % peers) for i in range(peers)]
    to_below = [(i, peers + (i - 1) % peers) for i in range(peers)]
    ring_below = lax.ppermute(f_high, ("tm", "space"), to_above)
    ring_above = lax.ppermute(f_low, ("tm", "space"), to_below)
    partner = lax.ppermute(partner, "tm", [(0, 1)])
    updated, = call(
        last_kernel, "update",
        (nodes, one, two, moved, work, below, above, h_low, h_high, partner, ring_below, ring_above),
        1, [(1, 3, planes, ny, nz)],
        [
            pltpu.VMEM((planes, halves, ny, LANES), F32),
            pltpu.VMEM((3, planes, halves, ny, LANES), F32),
            pltpu.SemaphoreType.DMA((halves,)),
            pltpu.SemaphoreType.DMA((3, planes, halves)),
        ],
        any_out=True, size=size * 6, flops=size * 5,
    )
    return updated


def solution(mesh):
    in_specs = (P(("groups", "tm"), None, "space", None, None),)
    out_specs = P(("groups", "tm"), None, "space", None, None)
    return jax.shard_map(local, mesh=mesh, in_specs=in_specs, out_specs=out_specs, check_vma=False)
```

```python
import jax
import jax.numpy as jnp
from jax import lax
from jax.experimental import pallas as pl
from jax.experimental.pallas import tpu as pltpu
from jax.sharding import PartitionSpec as P

DIFFUSE = 0.12
COARSE = DIFFUSE / 4.0
GROWTH = 0.5
WEIGHTS = ((5.0 / 24.0, 1.0 / 3.0, -1.0 / 24.0), (-1.0 / 24.0, 1.0 / 3.0, 5.0 / 24.0))
SECOND = (WEIGHTS[1][0], WEIGHTS[1][1] - 0.5, WEIGHTS[1][2])
LANES = 128
F32 = jnp.float32
BF16 = jnp.bfloat16
VMEM_LIMIT = 32 * 1024 * 1024


def combine(weights, parts):
    return weights[0] * parts[0] + weights[1] * parts[1] + weights[2] * parts[2]


def cube(v):
    return v * v * v


def z_neighbours(halves):
    count = len(halves)
    lane = lax.broadcasted_iota(jnp.int32, halves[0].shape, 1)
    fwd = [pltpu.roll(v, 1, 1) for v in halves]
    back = [pltpu.roll(v, LANES - 1, 1) for v in halves]
    out = []
    for k in range(count):
        before = jnp.where(lane == 0, fwd[(k - 1) % count], fwd[k])
        after = jnp.where(lane == LANES - 1, back[(k + 1) % count], back[k])
        out.append(before + after)
    return out


def y_neighbours(other, parity):
    rows = other.shape[0]
    return other + pltpu.roll(other, 1 if parity == 0 else rows - 1, 0)


def laplace_planes(ref, plane, planes, halves):
    for parity in range(2):
        own = [ref[plane, h, parity] for h in range(halves)]
        side = z_neighbours(own)
        for h in range(halves):
            total = side[h] + y_neighbours(ref[plane, h, 1 - parity], parity) - 6.0 * own[h]
            if plane > 0:
                total = total + ref[plane - 1, h, parity]
            if plane < planes - 1:
                total = total + ref[plane + 1, h, parity]
            yield h, parity, own[h], total


def coarse_force(field):
    planes = len(field)
    out = []
    for p in range(planes):
        v = field[p]
        rows, lanes = v.shape
        total = pltpu.roll(v, 1, 0) + pltpu.roll(v, rows - 1, 0)
        total = total + pltpu.roll(v, 1, 1) + pltpu.roll(v, lanes - 1, 1) - 6.0 * v
        if p > 0:
            total = total + field[p - 1]
        if p < planes - 1:
            total = total + field[p + 1]
        out.append(COARSE * total + GROWTH * (v - cube(v)))
    return out


def split(v):
    high = v.astype(BF16)
    low = (v - high.astype(F32)).astype(BF16)
    return high, low


def pair_matrix(size):
    row = lax.broadcasted_iota(jnp.int32, (size, size // 2), 0)
    col = lax.broadcasted_iota(jnp.int32, (size, size // 2), 1)
    offset = lax.rem(row - 2 * col + size, size)
    inner = offset < 2
    outer = (offset == 2) | (offset == size - 1)
    sums = jnp.where(inner, 1.0, 0.0).astype(F32)
    bends = jnp.where(outer, 1.0, 0.0).astype(F32) - sums
    return sums.astype(BF16), bends.astype(BF16)


def spread_matrix(size):
    row = lax.broadcasted_iota(jnp.int32, (size, 2 * size), 0)
    col = lax.broadcasted_iota(jnp.int32, (size, 2 * size), 1)
    return jnp.where((col == 2 * row) | (col == 2 * row + 1), 1.0, 0.0).astype(F32).astype(BF16)


def times(v, matrix):
    high, low = split(v)
    return jnp.dot(high, matrix, preferred_element_type=F32) + jnp.dot(
        low, matrix, preferred_element_type=F32
    )


def restrict_field(ref, planes, halves):
    size = halves * LANES
    sums, bends = pair_matrix(size)

    def y_sum(p):
        return [ref[p, h, 0] + ref[p, h, 1] for h in range(halves)]

    means, forces = [], []
    flat = [y_sum(p) for p in range(planes)]
    for top in range(0, planes, 2):
        total, rest = [], []
        for h in range(halves):
            even = ref[top, h, 0] + ref[top + 1, h, 0]
            odd = ref[top, h, 1] + ref[top + 1, h, 1]
            both = even + odd
            rows = both.shape[0]
            flux = pltpu.roll(odd, 1, 0) + pltpu.roll(even, rows - 1, 0) - 2.0 * both
            if top > 0:
                flux = flux + flat[top - 1][h]
            if top + 2 < planes:
                flux = flux + flat[top + 2][h]
            cubes = cube(ref[top, h, 0]) + cube(ref[top + 1, h, 0])
            cubes = cubes + cube(ref[top, h, 1]) + cube(ref[top + 1, h, 1])
            total.append(both)
            rest.append(DIFFUSE * flux + GROWTH * (both - cubes))
        total = jnp.concatenate(total, axis=1)
        rest = jnp.concatenate(rest, axis=1)
        means.append(times(total, sums) * 0.125)
        forces.append((times(rest, sums) + DIFFUSE * times(total, bends)) * 0.125)
    edges = [times(jnp.concatenate(flat[p], axis=1), sums) for p in (0, planes - 1)]
    return means, forces, edges


def store_coarse(out, means, forces, edges):
    for k, parts in enumerate((means, forces, edges)):
        for p, v in enumerate(parts):
            out[k, p] = v


def outer_planes(planes):
    odd = lax.rem(lax.axis_index("space"), 2)
    return (1 - odd) * (planes - 1), odd * (planes - 1)


def edge_kernel(nodes, near, far, held, sem):
    planes, halves = nodes.shape[2], held.shape[2]
    copies = []
    for e, p in enumerate(outer_planes(planes)):
        for m in range(3):
            for h in range(halves):
                copies.append(
                    pltpu.make_async_copy(
                        nodes.at[0, m, p, :, pl.ds(h * LANES, LANES)],
                        held.at[e, m, h],
                        sem.at[e, m, h],
                    )
                )
    for copy in copies:
        copy.start()
    for copy in copies:
        copy.wait()
    rows = near.shape[2]
    for e, out in enumerate((near, far)):
        for h in range(halves):
            for q in range(2):
                parts = [held[e, m, h, pl.ds(q, rows, stride=2), :] for m in range(3)]
                out[h, q] = combine(WEIGHTS[0], parts)


def first_kernel(nodes, one, slope, rest, near, far, coarse, held, start, mix, sem):
    planes, halves = nodes.shape[2], held.shape[2]
    rows = one.shape[3]
    copies = [
        [
            pltpu.make_async_copy(
                nodes.at[0, m, p, :, pl.ds(h * LANES, LANES)], held.at[m, p, h], sem.at[m, p, h]
            )
            for m in range(3)
            for h in range(halves)
        ]
        for p in range(planes)
    ]
    for group in copies:
        for copy in group:
            copy.start()
    for p in range(planes):
        for copy in copies[p]:
            copy.wait()
        for h in range(halves):
            for q in range(2):
                parts = [held[m, p, h, pl.ds(q, rows, stride=2), :] for m in range(3)]
                cubes = [cube(v) for v in parts]
                a = combine(WEIGHTS[0], parts)
                d = combine(SECOND, parts)
                start[p, h, q] = parts[0]
                mix[p, h, q] = a
                slope[p, h, q] = d
                one[p, h, q] = parts[0] + GROWTH * (a - combine(WEIGHTS[0], cubes))
                rest[p, h, q] = GROWTH * (d - combine(SECOND, cubes))
    for p in range(planes):
        for h, q, _, laplace in laplace_planes(mix, p, planes, halves):
            one[p, h, q] = one[p, h, q] + DIFFUSE * laplace
    for p, out in zip(outer_planes(planes), (near, far)):
        out[...] = 0.5 * one[p] + slope[p]
    store_coarse(coarse, *restrict_field(start, planes, halves))


def second_kernel(one_in, slope, rest, near, far, own_near, own_far, one, two, coarse, mix):
    planes, halves = one_in.shape[0], one_in.shape[1]
    outer = outer_planes(planes)
    for p in range(1, planes - 1):
        one[p] = one_in[p]
    for p, halo in zip(outer, (near, far)):
        one[p] = one_in[p] + DIFFUSE * halo[...]
    for p in range(planes):
        mix[p] = 0.5 * one[p] + slope[p]
    for p in range(planes):
        for h, q, _, laplace in laplace_planes(mix, p, planes, halves):
            value = one[p, h, q]
            two[p, h, q] = (
                value + DIFFUSE * laplace + (0.5 * GROWTH) * (value - cube(value)) + rest[p, h, q]
            )
    for p, own in zip(outer, (own_near, own_far)):
        two[p] = two[p] + (0.5 * DIFFUSE * DIFFUSE) * own[...]
    store_coarse(coarse, *restrict_field(one, planes, halves))


def third_kernel(two_in, near, far, coarse_zero, coarse_one, two, send_near, send_far, work):
    planes, halves = two_in.shape[0], two_in.shape[1]
    later = lax.axis_index("tm").astype(F32)
    for p in range(1, planes - 1):
        two[p] = two_in[p]
    for p, halo in zip(outer_planes(planes), (near, far)):
        two[p] = two_in[p] + DIFFUSE * halo[...]
    means_two, forces_two, edges_two = restrict_field(two, planes, halves)
    half = planes // 2
    zero = [coarse_zero[0, p] for p in range(half)]
    mean_one = [coarse_one[0, p] for p in range(half)]
    force_zero = coarse_force(zero)
    force_one = coarse_force(mean_one)
    sweep_zero, sweep_one = [], []
    for p in range(half):
        parts = (coarse_zero[1, p], coarse_one[1, p], forces_two[p])
        sweep_zero.append(combine(WEIGHTS[0], parts))
        sweep_one.append(combine(WEIGHTS[1], parts))
    sends = []
    for e, p in enumerate((0, half - 1)):
        parts = (coarse_zero[2, e], coarse_one[2, e], edges_two[e])
        partial = sweep_zero[p] - mean_one[p] + (1.0 - later) * zero[p] - (0.5 * later) * force_zero[p]
        sends.append((
            (DIFFUSE / 8.0) * combine(WEIGHTS[0], parts) - (0.5 * COARSE * later) * zero[p],
            (DIFFUSE / 8.0) * combine(WEIGHTS[1], parts) + (0.5 * COARSE) * partial,
        ))
    for k in range(2):
        send_near[k], send_far[k] = low_high(sends[0][k], sends[1][k])
    for p in range(half):
        work[0, p] = zero[p]
        work[1, p] = mean_one[p]
        work[2, p] = means_two[p]
        work[3, p] = sweep_zero[p] - 0.5 * force_zero[p]
        work[4, p] = sweep_one[p] - 0.5 * force_one[p]


def low_high(near, far):
    odd = lax.rem(lax.axis_index("space"), 2)
    return jnp.where(odd == 1, near, far), jnp.where(odd == 1, far, near)


def sides(near, far):
    pairs = [low_high(near[k], far[k]) for k in range(2)]
    return [v[0] for v in pairs], [v[1] for v in pairs]


def coarse_chain(first, first_low, first_high, bend_low, bend_high, work, low, high, own_low, own_high):
    half = len(first)
    force = coarse_force(first)
    one = []
    for p in range(half):
        v = first[p] + 0.5 * force[p] + work[3, p]
        if p == 0:
            v = v + low[0] + first_low
        if p == half - 1:
            v = v + high[0] + first_high
        one.append(v)
    force = coarse_force(one)
    two = []
    for p in range(half):
        v = one[p] + 0.5 * force[p] + work[4, p]
        if p == 0:
            v = v + low[1] + (0.5 * COARSE) * (own_low[0] + bend_low)
        if p == half - 1:
            v = v + high[1] + (0.5 * COARSE) * (own_high[0] + bend_high)
        two.append(v)
    return one, two


def fourth_kernel(work, near, far, own_near, own_far, held, partner, send_near, send_far, passed):
    del held, passed
    half = work.shape[1]
    first = [work[0, p] for p in range(half)]
    low, high = sides(near, far)
    own_low, own_high = sides(own_near, own_far)
    one, two = coarse_chain(first, 0.0, 0.0, 0.0, 0.0, work, low, high, own_low, own_high)
    force = coarse_force(two)
    for p in range(half):
        partner[0, p] = two[p]
        partner[1, p] = two[p] - work[2, p]
    send_near[0], send_far[0] = low_high(two[0], two[half - 1])
    send_near[1], send_far[1] = low_high(
        two[0] + 0.5 * force[0], two[half - 1] + 0.5 * force[half - 1]
    )


def last_kernel(
    nodes, one, two, moved, work, near, far, own_near, own_far, partner, ring_near, ring_far,
    updated, held, result, load_sem, store_sem,
):
    planes, halves = one.shape[0], one.shape[1]
    rows = one.shape[3]
    half = planes // 2
    section = lax.axis_index("tm")
    low, high = sides(near, far)
    own_low, own_high = sides(own_near, own_far)
    ring_low, ring_high = sides(ring_near, ring_far)
    loads = [
        pltpu.make_async_copy(
            nodes.at[0, 0, :, :, pl.ds(h * LANES, LANES)], held.at[:, h], load_sem.at[h]
        )
        for h in range(halves)
    ]
    for copy in loads:
        copy.start()
    first, change = [], []
    for p in range(half):
        first.append(jnp.where(section == 0, work[0, p], partner[0, p]))
        change.append(jnp.where(section == 0, first[p] - work[0, p], partner[1, p]))
    scale = 0.5 * COARSE
    coarse_one, coarse_two = coarse_chain(
        first,
        jnp.where(section == 0, 0.0, scale * ring_low[0]),
        jnp.where(section == 0, 0.0, scale * ring_high[0]),
        jnp.where(section == 0, 0.0, ring_low[1] + scale * first[0]),
        jnp.where(section == 0, 0.0, ring_high[1] + scale * first[half - 1]),
        work, low, high, own_low, own_high,
    )
    spread = spread_matrix(LANES * halves // 2)
    stores = []

    def put(node, p):
        for h in range(halves):
            copy = pltpu.make_async_copy(
                result.at[node, p, h],
                updated.at[0, node, p, :, pl.ds(h * LANES, LANES)],
                store_sem.at[node, p, h],
            )
            copy.start()
            stores.append(copy)

    for node, base in ((1, one), (2, two)):
        for top in range(half):
            diff = (coarse_one[top] if node == 1 else coarse_two[top]) - work[node, top]
            wide = times(diff, spread)
            for p in (2 * top, 2 * top + 1):
                for h in range(halves):
                    for q in range(2):
                        result[node, p, h, pl.ds(q, rows, stride=2), :] = (
                            base[p, h, q] + wide[:, h * LANES : (h + 1) * LANES]
                        )
                put(node, p)
    for copy in loads:
        copy.wait()
    for top in range(half):
        wide = times(change[top], spread)
        for p in (2 * top, 2 * top + 1):
            for h in range(halves):
                for q in range(2):
                    own = held[p, h, pl.ds(q, rows, stride=2), :]
                    start = jnp.where(section == 0, own, moved[p, h, q])
                    result[0, p, h, pl.ds(q, rows, stride=2), :] = (
                        start + wide[:, h * LANES : (h + 1) * LANES]
                    )
            put(0, p)
    for copy in stores:
        copy.wait()


def call(kernel, name, inputs, any_inputs, outs, scratch=(), any_outs=(), limit=VMEM_LIMIT,
         aliases=None, flops=0, size=0):
    def spec(far, passed):
        return pl.BlockSpec(
            memory_space=pl.ANY if passed else pltpu.HBM if far else pltpu.VMEM
        )

    return pl.pallas_call(
        kernel,
        name=name,
        out_shape=[jax.ShapeDtypeStruct(s, F32) for s in outs],
        in_specs=[spec(k in any_inputs, k in (aliases or {})) for k in range(len(inputs))],
        out_specs=[spec(k in any_outs, k in (aliases or {}).values()) for k in range(len(outs))],
        scratch_shapes=list(scratch),
        input_output_aliases=aliases or {},
        compiler_params=pltpu.CompilerParams(vmem_limit_bytes=limit),
        cost_estimate=pl.CostEstimate(flops=flops, bytes_accessed=size, transcendentals=0),
    )(*inputs)


def pairings(peers):
    near = [i ^ 1 for i in range(peers)]
    far = [(i + 1) % peers if i % 2 else (i - 1) % peers for i in range(peers)]
    return near, far


def exchange(near, far):
    to_near, to_far = pairings(lax.axis_size("space"))
    return (
        lax.ppermute(near, "space", list(enumerate(to_near))),
        lax.ppermute(far, "space", list(enumerate(to_far))),
    )


def swapped(value):
    return lax.ppermute(value, "tm", [(0, 1), (1, 0)])


def handed_on(near, far):
    peers = lax.axis_size("space")
    out = []
    for value, to in zip((near, far), pairings(peers)):
        perm = [(i, peers + to[i]) for i in range(peers)] + [(peers + i, i) for i in range(peers)]
        out.append(lax.ppermute(value, ("tm", "space"), perm))
    return out


def local(nodes):
    _, _, planes, ny, nz = nodes.shape
    halves, rows, half = nz // LANES, ny // 2, planes // 2
    plane = (halves, 2, rows, LANES)
    field = (planes,) + plane
    quarter = (rows, nz // 2)
    pair = (2,) + quarter
    packed = (3, half) + quarter
    size = planes * ny * nz * 4

    a_near, a_far = call(
        edge_kernel, "edge_mix", (nodes,), (0,), [plane, plane],
        [pltpu.VMEM((2, 3, halves, ny, LANES), F32), pltpu.SemaphoreType.DMA((2, 3, halves))],
        size=size * 2, flops=size,
    )
    got_a_near, got_a_far = exchange(a_near, a_far)
    one_part, slope, rest, b_near, b_far, coarse_zero = call(
        first_kernel, "first_stage", (nodes,), (0,), [field, field, field, plane, plane, packed],
        [
            pltpu.VMEM((3, planes, halves, ny, LANES), F32),
            pltpu.VMEM(field, F32),
            pltpu.VMEM(field, F32),
            pltpu.SemaphoreType.DMA((3, planes, halves)),
        ],
        size=size * 6, flops=size * 10,
    )
    got_b_near, got_b_far = exchange(b_near, b_far)
    one, two_part, coarse_mid = call(
        second_kernel, "second_stage",
        (one_part, slope, rest, got_a_near, got_a_far, a_near, a_far), (),
        [field, field, packed], [pltpu.VMEM(field, F32)],
        size=size * 6, flops=size * 10,
    )
    two, h_near, h_far, work = call(
        third_kernel, "third_stage", (two_part, got_b_near, got_b_far, coarse_zero, coarse_mid), (),
        [field, pair, pair, (5, half) + quarter],
        size=size * 3, flops=size * 5,
    )
    got_near, got_far = exchange(h_near, h_far)
    partner, f_near, f_far, two = call(
        fourth_kernel, "coarse_chain", (work, got_near, got_far, h_near, h_far, two), (5,),
        [(2, half) + quarter, pair, pair, field], any_outs=(3,), aliases={5: 3},
        size=size, flops=size,
    )
    ring_near, ring_far = handed_on(f_near, f_far)
    partner = swapped(partner)
    moved = swapped(two)
    updated, = call(
        last_kernel, "update",
        (nodes, one, two, moved, work, got_near, got_far, h_near, h_far, partner, ring_near, ring_far),
        (0,), [(1, 3, planes, ny, nz)],
        [
            pltpu.VMEM((planes, halves, ny, LANES), F32),
            pltpu.VMEM((3, planes, halves, ny, LANES), F32),
            pltpu.SemaphoreType.DMA((halves,)),
            pltpu.SemaphoreType.DMA((3, planes, halves)),
        ],
        any_outs=(0,), size=size * 6, flops=size * 5,
    )
    return updated


def solution(mesh):
    in_specs = (P(("groups", "tm"), None, "space", None, None),)
    out_specs = P(("groups", "tm"), None, "space", None, None)
    return jax.shard_map(local, mesh=mesh, in_specs=in_specs, out_specs=out_specs, check_vma=False)
```

```python
import jax
import jax.numpy as jnp
from jax import lax
from jax.experimental import pallas as pl
from jax.experimental.pallas import tpu as pltpu
from jax.sharding import PartitionSpec as P

DIFFUSE = 0.12
COARSE = DIFFUSE / 4.0
GROWTH = 0.5
WEIGHTS = ((5.0 / 24.0, 1.0 / 3.0, -1.0 / 24.0), (-1.0 / 24.0, 1.0 / 3.0, 5.0 / 24.0))
SECOND = (WEIGHTS[1][0], WEIGHTS[1][1] - 0.5, WEIGHTS[1][2])
LANES = 128
F32 = jnp.float32
BF16 = jnp.bfloat16
VMEM_LIMIT = 32 * 1024 * 1024
EDGE_LIMIT = 52 * 1024 * 1024
FIRST_LIMIT = 48 * 1024 * 1024


def combine(weights, parts):
    return weights[0] * parts[0] + weights[1] * parts[1] + weights[2] * parts[2]


def cube(v):
    return v * v * v


def z_neighbours(halves):
    count = len(halves)
    lane = lax.broadcasted_iota(jnp.int32, halves[0].shape, 1)
    fwd = [pltpu.roll(v, 1, 1) for v in halves]
    back = [pltpu.roll(v, LANES - 1, 1) for v in halves]
    out = []
    for k in range(count):
        before = jnp.where(lane == 0, fwd[(k - 1) % count], fwd[k])
        after = jnp.where(lane == LANES - 1, back[(k + 1) % count], back[k])
        out.append(before + after)
    return out


def y_neighbours(other, parity):
    rows = other.shape[0]
    return other + pltpu.roll(other, 1 if parity == 0 else rows - 1, 0)


def laplace_planes(ref, plane, planes, halves):
    for parity in range(2):
        own = [ref[plane, h, parity] for h in range(halves)]
        side = z_neighbours(own)
        for h in range(halves):
            total = side[h] + y_neighbours(ref[plane, h, 1 - parity], parity) - 6.0 * own[h]
            if plane > 0:
                total = total + ref[plane - 1, h, parity]
            if plane < planes - 1:
                total = total + ref[plane + 1, h, parity]
            yield h, parity, own[h], total


def coarse_force(field):
    planes = len(field)
    out = []
    for p in range(planes):
        v = field[p]
        rows, lanes = v.shape
        total = pltpu.roll(v, 1, 0) + pltpu.roll(v, rows - 1, 0)
        total = total + pltpu.roll(v, 1, 1) + pltpu.roll(v, lanes - 1, 1) - 6.0 * v
        if p > 0:
            total = total + field[p - 1]
        if p < planes - 1:
            total = total + field[p + 1]
        out.append(COARSE * total + GROWTH * (v - cube(v)))
    return out


def split(v):
    high = v.astype(BF16)
    low = (v - high.astype(F32)).astype(BF16)
    return high, low


def pair_matrix(size):
    row = lax.broadcasted_iota(jnp.int32, (size, size // 2), 0)
    col = lax.broadcasted_iota(jnp.int32, (size, size // 2), 1)
    offset = lax.rem(row - 2 * col + size, size)
    inner = offset < 2
    outer = (offset == 2) | (offset == size - 1)
    sums = jnp.where(inner, 1.0, 0.0).astype(F32)
    bends = jnp.where(outer, 1.0, 0.0).astype(F32) - sums
    return sums.astype(BF16), bends.astype(BF16)


def spread_matrix(size):
    row = lax.broadcasted_iota(jnp.int32, (size, 2 * size), 0)
    col = lax.broadcasted_iota(jnp.int32, (size, 2 * size), 1)
    return jnp.where((col == 2 * row) | (col == 2 * row + 1), 1.0, 0.0).astype(F32).astype(BF16)


def times(v, matrix):
    high, low = split(v)
    return jnp.dot(high, matrix, preferred_element_type=F32) + jnp.dot(
        low, matrix, preferred_element_type=F32
    )


def restrict_field(ref, planes, halves):
    size = halves * LANES
    sums, bends = pair_matrix(size)

    def y_sum(p):
        return [ref[p, h, 0] + ref[p, h, 1] for h in range(halves)]

    means, forces = [], []
    flat = [y_sum(p) for p in range(planes)]
    for top in range(0, planes, 2):
        total, rest = [], []
        for h in range(halves):
            even = ref[top, h, 0] + ref[top + 1, h, 0]
            odd = ref[top, h, 1] + ref[top + 1, h, 1]
            both = even + odd
            rows = both.shape[0]
            flux = pltpu.roll(odd, 1, 0) + pltpu.roll(even, rows - 1, 0) - 2.0 * both
            if top > 0:
                flux = flux + flat[top - 1][h]
            if top + 2 < planes:
                flux = flux + flat[top + 2][h]
            cubes = cube(ref[top, h, 0]) + cube(ref[top + 1, h, 0])
            cubes = cubes + cube(ref[top, h, 1]) + cube(ref[top + 1, h, 1])
            total.append(both)
            rest.append(DIFFUSE * flux + GROWTH * (both - cubes))
        total = jnp.concatenate(total, axis=1)
        rest = jnp.concatenate(rest, axis=1)
        means.append(times(total, sums) * 0.125)
        forces.append((times(rest, sums) + DIFFUSE * times(total, bends)) * 0.125)
    edges = [times(jnp.concatenate(flat[p], axis=1), sums) for p in (0, planes - 1)]
    return means, forces, edges


def store_coarse(out, means, forces, edges):
    for k, parts in enumerate((means, forces, edges)):
        for p, v in enumerate(parts):
            out[k, p] = v


def outer_planes(planes):
    odd = lax.rem(lax.axis_index("space"), 2)
    return (1 - odd) * (planes - 1), odd * (planes - 1)


def edge_kernel(nodes, near, far, held, work, sem):
    planes, halves = nodes.shape[2], near.shape[0]
    rows = near.shape[2]
    copies = [
        [
            pltpu.make_async_copy(nodes.at[0, m, p], held.at[e, m], sem.at[e, m])
            for m in range(3)
        ]
        for e, p in enumerate(outer_planes(planes))
    ]
    for group in copies:
        for copy in group:
            copy.start()
    for e, out in enumerate((near, far)):
        for copy in copies[e]:
            copy.wait()
        for h in range(halves):
            lanes = pl.ds(h * LANES, LANES)
            work[e, h] = combine(WEIGHTS[0], [held[e, m, :, lanes] for m in range(3)])
            for q in range(2):
                out[h, q] = work[e, h, pl.ds(q, rows, stride=2), :]


def first_kernel(nodes, one, slope, rest, near, far, coarse, work, start, mix):
    planes, halves = one.shape[0], one.shape[1]
    rows = one.shape[3]
    for p in range(planes):
        for h in range(halves):
            lanes = pl.ds(h * LANES, LANES)
            parts = [nodes[0, m, p, :, lanes] for m in range(3)]
            cubes = [cube(v) for v in parts]
            a = combine(WEIGHTS[0], parts)
            d = combine(SECOND, parts)
            work[0] = parts[0]
            work[1] = a
            work[2] = d
            work[3] = parts[0] + GROWTH * (a - combine(WEIGHTS[0], cubes))
            work[4] = GROWTH * (d - combine(SECOND, cubes))
            for q in range(2):
                for k, out in enumerate((start, mix, slope, one, rest)):
                    out[p, h, q] = work[k, pl.ds(q, rows, stride=2), :]
    for p in range(planes):
        for h, q, _, laplace in laplace_planes(mix, p, planes, halves):
            one[p, h, q] = one[p, h, q] + DIFFUSE * laplace
    for p, out in zip(outer_planes(planes), (near, far)):
        out[...] = 0.5 * one[p] + slope[p]
    store_coarse(coarse, *restrict_field(start, planes, halves))


def second_kernel(one_in, slope, rest, near, far, own_near, own_far, one, two, coarse, mix):
    planes, halves = one_in.shape[0], one_in.shape[1]
    outer = outer_planes(planes)
    for p in range(1, planes - 1):
        one[p] = one_in[p]
    for p, halo in zip(outer, (near, far)):
        one[p] = one_in[p] + DIFFUSE * halo[...]
    for p in range(planes):
        mix[p] = 0.5 * one[p] + slope[p]
    for p in range(planes):
        for h, q, _, laplace in laplace_planes(mix, p, planes, halves):
            value = one[p, h, q]
            two[p, h, q] = (
                value + DIFFUSE * laplace + (0.5 * GROWTH) * (value - cube(value)) + rest[p, h, q]
            )
    for p, own in zip(outer, (own_near, own_far)):
        two[p] = two[p] + (0.5 * DIFFUSE * DIFFUSE) * own[...]
    store_coarse(coarse, *restrict_field(one, planes, halves))


def third_kernel(two_in, near, far, coarse_zero, coarse_one, two, send_near, send_far, work):
    planes, halves = two_in.shape[0], two_in.shape[1]
    later = lax.axis_index("tm").astype(F32)
    for p in range(1, planes - 1):
        two[p] = two_in[p]
    for p, halo in zip(outer_planes(planes), (near, far)):
        two[p] = two_in[p] + DIFFUSE * halo[...]
    means_two, forces_two, edges_two = restrict_field(two, planes, halves)
    half = planes // 2
    zero = [coarse_zero[0, p] for p in range(half)]
    mean_one = [coarse_one[0, p] for p in range(half)]
    force_zero = coarse_force(zero)
    force_one = coarse_force(mean_one)
    sweep_zero, sweep_one = [], []
    for p in range(half):
        parts = (coarse_zero[1, p], coarse_one[1, p], forces_two[p])
        sweep_zero.append(combine(WEIGHTS[0], parts))
        sweep_one.append(combine(WEIGHTS[1], parts))
    sends = []
    for e, p in enumerate((0, half - 1)):
        parts = (coarse_zero[2, e], coarse_one[2, e], edges_two[e])
        partial = sweep_zero[p] - mean_one[p] + (1.0 - later) * zero[p] - (0.5 * later) * force_zero[p]
        sends.append((
            (DIFFUSE / 8.0) * combine(WEIGHTS[0], parts) - (0.5 * COARSE * later) * zero[p],
            (DIFFUSE / 8.0) * combine(WEIGHTS[1], parts) + (0.5 * COARSE) * partial,
        ))
    for k in range(2):
        send_near[k], send_far[k] = low_high(sends[0][k], sends[1][k])
    for p in range(half):
        work[0, p] = zero[p]
        work[1, p] = mean_one[p]
        work[2, p] = means_two[p]
        work[3, p] = sweep_zero[p] - 0.5 * force_zero[p]
        work[4, p] = sweep_one[p] - 0.5 * force_one[p]
        two[planes, 0, p] = means_two[p]


def low_high(near, far):
    odd = lax.rem(lax.axis_index("space"), 2)
    return jnp.where(odd == 1, near, far), jnp.where(odd == 1, far, near)


def sides(near, far):
    pairs = [low_high(near[k], far[k]) for k in range(2)]
    return [v[0] for v in pairs], [v[1] for v in pairs]


def with_halo(work, low, high, own_low, own_high):
    half = work.shape[1]
    one = [work[3, p] for p in range(half)]
    two = [work[4, p] for p in range(half)]
    for p, got, own in ((0, low, own_low), (half - 1, high, own_high)):
        one[p] = one[p] + got[0]
        two[p] = two[p] + got[1] + (0.5 * COARSE) * own[0]
    return one, two


def coarse_steps(first, ends, bends, sweep_one, sweep_two):
    half = len(first)
    force = coarse_force(first)
    one = [first[p] + 0.5 * force[p] + sweep_one[p] for p in range(half)]
    for p, end in zip((0, half - 1), ends):
        one[p] = one[p] + end
    force = coarse_force(one)
    two = [one[p] + 0.5 * force[p] + sweep_two[p] for p in range(half)]
    for p, bend in zip((0, half - 1), bends):
        two[p] = two[p] + (0.5 * COARSE) * bend
    return one, two


def fourth_kernel(work, near, far, own_near, own_far, end, send_near, send_far, swept):
    half = work.shape[1]
    first = [work[0, p] for p in range(half)]
    low, high = sides(near, far)
    own_low, own_high = sides(own_near, own_far)
    sweeps = with_halo(work, low, high, own_low, own_high)
    _, two = coarse_steps(first, (0.0, 0.0), (0.0, 0.0), *sweeps)
    for k, parts in enumerate(sweeps):
        for p in range(half):
            swept[k, p] = parts[p]
    force = coarse_force(two)
    for p in range(half):
        end[p] = two[p]
    send_near[0], send_far[0] = low_high(two[0], two[half - 1])
    send_near[1], send_far[1] = low_high(
        two[0] + 0.5 * force[0], two[half - 1] + 0.5 * force[half - 1]
    )


def last_kernel(
    nodes, ring_far, ring_near, end, one, two, moved, work, swept,
    updated, held, result, load_sem, store_sem,
):
    planes, halves = one.shape[0], one.shape[1]
    rows = one.shape[3]
    half = planes // 2
    section = lax.axis_index("tm")
    loads = [
        pltpu.make_async_copy(
            nodes.at[0, 0, :, :, pl.ds(h * LANES, LANES)], held.at[:, h], load_sem.at[h]
        )
        for h in range(halves)
    ]
    for copy in loads:
        copy.start()
    spread = spread_matrix(LANES * halves // 2)
    first = [jnp.where(section == 0, work[0, p], end[p]) for p in range(half)]
    stores = []

    def put(node, top, change, base):
        wide = times(change, spread)
        for p in (2 * top, 2 * top + 1):
            for h in range(halves):
                for q in range(2):
                    result[node, p, h, pl.ds(q, rows, stride=2), :] = (
                        base(p, h, q) + wide[:, h * LANES : (h + 1) * LANES]
                    )
                copy = pltpu.make_async_copy(
                    result.at[node, p, h],
                    updated.at[0, node, p, :, pl.ds(h * LANES, LANES)],
                    store_sem.at[node, p, h],
                )
                copy.start()
                stores.append(copy)

    def start(p, h, q):
        own = held[p, h, pl.ds(q, rows, stride=2), :]
        return jnp.where(section == 0, own, moved[p, h, q])

    for copy in loads:
        copy.wait()
    for top in range(half):
        mean = jnp.where(section == 0, work[0, top], moved[planes, 0, top])
        put(0, top, first[top] - mean, start)

    ring_low, ring_high = sides(ring_near, ring_far)
    scale = 0.5 * COARSE
    ends = [jnp.where(section == 0, 0.0, scale * v[0]) for v in (ring_low, ring_high)]
    bends = [
        jnp.where(section == 0, 0.0, v[1] + scale * first[p])
        for v, p in ((ring_low, 0), (ring_high, half - 1))
    ]
    coarse_one, coarse_two = coarse_steps(
        first, ends, bends, *[[swept[k, p] for p in range(half)] for k in range(2)]
    )
    for top in range(half):
        put(1, top, coarse_one[top] - work[1, top], lambda p, h, q: one[p, h, q])
    for top in range(half):
        put(2, top, coarse_two[top] - work[2, top], lambda p, h, q: two[p, h, q])
    for copy in stores:
        copy.wait()


def call(kernel, name, inputs, any_inputs, outs, scratch=(), any_outs=(), limit=VMEM_LIMIT,
         aliases=None, flops=0, size=0):
    def spec(far):
        return pl.BlockSpec(memory_space=pl.ANY if far else pltpu.VMEM)

    return pl.pallas_call(
        kernel,
        name=name,
        out_shape=[jax.ShapeDtypeStruct(s, F32) for s in outs],
        in_specs=[spec(k in any_inputs) for k in range(len(inputs))],
        out_specs=[spec(k in any_outs) for k in range(len(outs))],
        scratch_shapes=list(scratch),
        input_output_aliases=aliases or {},
        compiler_params=pltpu.CompilerParams(vmem_limit_bytes=limit),
        cost_estimate=pl.CostEstimate(flops=flops, bytes_accessed=size, transcendentals=0),
    )(*inputs)


def pairings(peers):
    near = [i ^ 1 for i in range(peers)]
    far = [(i + 1) % peers if i % 2 else (i - 1) % peers for i in range(peers)]
    return near, far


def exchange(near, far):
    to_near, to_far = pairings(lax.axis_size("space"))
    return (
        lax.ppermute(near, "space", list(enumerate(to_near))),
        lax.ppermute(far, "space", list(enumerate(to_far))),
    )


def swapped(value):
    return lax.ppermute(value, "tm", [(0, 1), (1, 0)])


def handed_on(near, far):
    peers = lax.axis_size("space")
    out = []
    for value, to in zip((far, near), pairings(peers)[::-1]):
        perm = [(i, peers + to[i]) for i in range(peers)] + [(peers + i, i) for i in range(peers)]
        out.append(lax.ppermute(value, ("tm", "space"), perm))
    return out


def local(nodes):
    _, _, planes, ny, nz = nodes.shape
    halves, rows, half = nz // LANES, ny // 2, planes // 2
    plane = (halves, 2, rows, LANES)
    field = (planes,) + plane
    quarter = (rows, nz // 2)
    pair = (2,) + quarter
    packed = (3, half) + quarter
    size = planes * ny * nz * 4

    a_near, a_far = call(
        edge_kernel, "edge_mix", (nodes,), (0,), [plane, plane],
        [
            pltpu.VMEM((2, 3, ny, nz), F32),
            pltpu.VMEM((2, halves, ny, LANES), F32),
            pltpu.SemaphoreType.DMA((2, 3)),
        ],
        limit=EDGE_LIMIT, size=size * 2, flops=size,
    )
    got_a_near, got_a_far = exchange(a_near, a_far)
    one_part, slope, rest, b_near, b_far, coarse_zero = call(
        first_kernel, "first_stage", (nodes,), (), [field, field, field, plane, plane, packed],
        [pltpu.VMEM((5, ny, LANES), F32), pltpu.VMEM(field, F32), pltpu.VMEM(field, F32)],
        limit=FIRST_LIMIT,
        size=size * 6, flops=size * 10,
    )
    got_b_near, got_b_far = exchange(b_near, b_far)
    one, two_part, coarse_mid = call(
        second_kernel, "second_stage",
        (one_part, slope, rest, got_a_near, got_a_far, a_near, a_far), (),
        [field, field, packed], [pltpu.VMEM(field, F32)],
        size=size * 6, flops=size * 10,
    )
    two, h_near, h_far, work = call(
        third_kernel, "third_stage", (two_part, got_b_near, got_b_far, coarse_zero, coarse_mid), (),
        [(planes + 1,) + plane, pair, pair, (5, half) + quarter],
        size=size * 3, flops=size * 5,
    )
    moved = swapped(two)
    got_near, got_far = exchange(h_near, h_far)
    end, f_near, f_far, swept = call(
        fourth_kernel, "coarse_chain", (work, got_near, got_far, h_near, h_far), (),
        [(half,) + quarter, pair, pair, (2, half) + quarter], size=size, flops=size,
    )
    ring_far, ring_near = handed_on(f_near, f_far)
    end = swapped(end)
    updated, = call(
        last_kernel, "update",
        (nodes, ring_far, ring_near, end, one, two, moved, work, swept),
        (0,), [(1, 3, planes, ny, nz)],
        [
            pltpu.VMEM((planes, halves, ny, LANES), F32),
            pltpu.VMEM((3, planes, halves, ny, LANES), F32),
            pltpu.SemaphoreType.DMA((halves,)),
            pltpu.SemaphoreType.DMA((3, planes, halves)),
        ],
        any_outs=(0,), size=size * 6, flops=size * 5,
    )
    return updated


def solution(mesh):
    in_specs = (P(("groups", "tm"), None, "space", None, None),)
    out_specs = P(("groups", "tm"), None, "space", None, None)
    return jax.shard_map(local, mesh=mesh, in_specs=in_specs, out_specs=out_specs, check_vma=False)
```

```python
import jax
import jax.numpy as jnp
import numpy as np
from jax import lax
from jax.experimental import pallas as pl
from jax.experimental.pallas import tpu as pltpu
from jax.sharding import PartitionSpec as P

DIFFUSE = 0.12
COARSE = DIFFUSE / 4.0
GROWTH = 0.5
WEIGHTS = ((5.0 / 24.0, 1.0 / 3.0, -1.0 / 24.0), (-1.0 / 24.0, 1.0 / 3.0, 5.0 / 24.0))
SECOND = (WEIGHTS[1][0], WEIGHTS[1][1] - 0.5, WEIGHTS[1][2])
LANES = 128
F32 = jnp.float32
BF16 = jnp.bfloat16
VMEM_LIMIT = 32 * 1024 * 1024
EDGE_LIMIT = 52 * 1024 * 1024
FIRST_LIMIT = 48 * 1024 * 1024


def combine(weights, parts):
    return weights[0] * parts[0] + weights[1] * parts[1] + weights[2] * parts[2]


def cube(v):
    return v * v * v


def z_neighbours(halves):
    count = len(halves)
    lane = lax.broadcasted_iota(jnp.int32, halves[0].shape, 1)
    fwd = [pltpu.roll(v, 1, 1) for v in halves]
    back = [pltpu.roll(v, LANES - 1, 1) for v in halves]
    out = []
    for k in range(count):
        before = jnp.where(lane == 0, fwd[(k - 1) % count], fwd[k])
        after = jnp.where(lane == LANES - 1, back[(k + 1) % count], back[k])
        out.append(before + after)
    return out


def y_neighbours(other, parity):
    rows = other.shape[0]
    return other + pltpu.roll(other, 1 if parity == 0 else rows - 1, 0)


def laplace_planes(ref, plane, planes, halves):
    for parity in range(2):
        own = [ref[plane, h, parity] for h in range(halves)]
        side = z_neighbours(own)
        for h in range(halves):
            total = side[h] + y_neighbours(ref[plane, h, 1 - parity], parity) - 6.0 * own[h]
            if plane > 0:
                total = total + ref[plane - 1, h, parity]
            if plane < planes - 1:
                total = total + ref[plane + 1, h, parity]
            yield h, parity, own[h], total


def coarse_force(field):
    planes = len(field)
    out = []
    for p in range(planes):
        v = field[p]
        rows, lanes = v.shape
        total = pltpu.roll(v, 1, 0) + pltpu.roll(v, rows - 1, 0)
        total = total + pltpu.roll(v, 1, 1) + pltpu.roll(v, lanes - 1, 1) - 6.0 * v
        if p > 0:
            total = total + field[p - 1]
        if p < planes - 1:
            total = total + field[p + 1]
        out.append(COARSE * total + GROWTH * (v - cube(v)))
    return out


def split(v):
    high = v.astype(BF16)
    low = (v - high.astype(F32)).astype(BF16)
    return high, low


def pair_matrix(size):
    out = np.zeros((size, size), np.float32)
    for k in range(size // 2):
        for offset in (0, 1):
            out[2 * k + offset, k] = 1.0
            out[2 * k + offset, size // 2 + k] = -1.0
        for offset in (-1, 2):
            out[(2 * k + offset) % size, size // 2 + k] = 1.0
    return jnp.asarray(out, BF16)


def spread_matrix(size):
    return jnp.asarray(np.repeat(np.eye(size, dtype=np.float32), 2, axis=1), BF16)


def times(v, matrix):
    high, low = split(v)
    return jnp.dot(high, matrix, preferred_element_type=F32) + jnp.dot(
        low, matrix, preferred_element_type=F32
    )


def restrict_field(ref, pairs, planes, halves):
    sums, bends = pairs[:, : halves * LANES // 2], pairs[:, halves * LANES // 2 :]

    def y_sum(p):
        return [ref[p, h, 0] + ref[p, h, 1] for h in range(halves)]

    means, forces = [], []
    flat = [y_sum(p) for p in range(planes)]
    for top in range(0, planes, 2):
        total, rest = [], []
        for h in range(halves):
            even = ref[top, h, 0] + ref[top + 1, h, 0]
            odd = ref[top, h, 1] + ref[top + 1, h, 1]
            both = even + odd
            rows = both.shape[0]
            flux = pltpu.roll(odd, 1, 0) + pltpu.roll(even, rows - 1, 0) - 2.0 * both
            if top > 0:
                flux = flux + flat[top - 1][h]
            if top + 2 < planes:
                flux = flux + flat[top + 2][h]
            cubes = cube(ref[top, h, 0]) + cube(ref[top + 1, h, 0])
            cubes = cubes + cube(ref[top, h, 1]) + cube(ref[top + 1, h, 1])
            total.append(both)
            rest.append(DIFFUSE * flux + GROWTH * (both - cubes))
        total = jnp.concatenate(total, axis=1)
        rest = jnp.concatenate(rest, axis=1)
        means.append(times(total, sums) * 0.125)
        forces.append((times(rest, sums) + DIFFUSE * times(total, bends)) * 0.125)
    edges = [times(jnp.concatenate(flat[p], axis=1), sums) for p in (0, planes - 1)]
    return means, forces, edges


def store_coarse(out, means, forces, edges):
    for k, parts in enumerate((means, forces, edges)):
        for p, v in enumerate(parts):
            out[k, p] = v


def outer_planes(planes):
    odd = lax.rem(lax.axis_index("space"), 2)
    return (1 - odd) * (planes - 1), odd * (planes - 1)


def edge_kernel(nodes, near, far, held, work, sem):
    planes, halves = nodes.shape[2], near.shape[0]
    rows = near.shape[2]
    copies = [
        [
            pltpu.make_async_copy(nodes.at[0, m, p], held.at[e, m], sem.at[e, m])
            for m in range(3)
        ]
        for e, p in enumerate(outer_planes(planes))
    ]
    for group in copies:
        for copy in group:
            copy.start()
    for e, out in enumerate((near, far)):
        for copy in copies[e]:
            copy.wait()
        for h in range(halves):
            lanes = pl.ds(h * LANES, LANES)
            work[e, h] = combine(WEIGHTS[0], [held[e, m, :, lanes] for m in range(3)])
            for q in range(2):
                out[h, q] = work[e, h, pl.ds(q, rows, stride=2), :]


def first_kernel(nodes, pairs, one, slope, rest, near, far, coarse, work, start, mix):
    planes, halves = one.shape[0], one.shape[1]
    rows = one.shape[3]
    for p in range(planes):
        for h in range(halves):
            lanes = pl.ds(h * LANES, LANES)
            parts = [nodes[0, m, p, :, lanes] for m in range(3)]
            cubes = [cube(v) for v in parts]
            a = combine(WEIGHTS[0], parts)
            d = combine(SECOND, parts)
            work[0] = parts[0]
            work[1] = a
            work[2] = d
            work[3] = parts[0] + GROWTH * (a - combine(WEIGHTS[0], cubes))
            work[4] = GROWTH * (d - combine(SECOND, cubes))
            for q in range(2):
                for k, out in enumerate((start, mix, slope, one, rest)):
                    out[p, h, q] = work[k, pl.ds(q, rows, stride=2), :]
    for p in range(planes):
        for h, q, _, laplace in laplace_planes(mix, p, planes, halves):
            one[p, h, q] = one[p, h, q] + DIFFUSE * laplace
    for p, out in zip(outer_planes(planes), (near, far)):
        out[...] = 0.5 * one[p] + slope[p]
    store_coarse(coarse, *restrict_field(start, pairs, planes, halves))


def second_kernel(
    one_in, slope, rest, near, far, own_near, own_far, pairs, one, two, coarse, inner, mix
):
    planes, halves = one_in.shape[0], one_in.shape[1]
    outer = outer_planes(planes)
    for p in range(1, planes - 1):
        one[p] = one_in[p]
    for p, halo in zip(outer, (near, far)):
        one[p] = one_in[p] + DIFFUSE * halo[...]
    for p in range(planes):
        mix[p] = 0.5 * one[p] + slope[p]
    for p in range(planes):
        for h, q, _, laplace in laplace_planes(mix, p, planes, halves):
            value = one[p, h, q]
            two[p, h, q] = (
                value + DIFFUSE * laplace + (0.5 * GROWTH) * (value - cube(value)) + rest[p, h, q]
            )
    for p, own in zip(outer, (own_near, own_far)):
        two[p] = two[p] + (0.5 * DIFFUSE * DIFFUSE) * own[...]
    for k, p in enumerate((1, planes - 2)):
        for h in range(halves):
            even, odd = two[p, h, 0], two[p, h, 1]
            inner[k, 0, h] = even
            inner[k, 1, h] = odd
            inner[k, 2, h] = GROWTH * (even + odd - cube(even) - cube(odd))
    store_coarse(coarse, *restrict_field(one, pairs, planes, halves))


def third_kernel(
    two_in, near, far, inner, coarse_zero, coarse_one, pairs, two, send_near, send_far, work, outer
):
    planes, halves = two_in.shape[0] - 1, two_in.shape[1]
    later = lax.axis_index("tm").astype(F32)
    for p, halo in zip(outer_planes(planes), (near, far)):
        outer[p // (planes - 1)] = two_in[p] + DIFFUSE * halo[...]
    totals, rests, flats = [], [], []
    other_flats = [[inner[k, 0, h] + inner[k, 1, h] for h in range(halves)] for k in range(2)]
    for k in range(2):
        two[k * (planes - 1)] = outer[k]
        total, rest, flat = [], [], []
        for h in range(halves):
            own = outer[k, h, 0], outer[k, h, 1]
            even, odd = own[0] + inner[k, 0, h], own[1] + inner[k, 1, h]
            line = own[0] + own[1]
            full = line + other_flats[k][h]
            rows = full.shape[0]
            flux = pltpu.roll(odd, 1, 0) + pltpu.roll(even, rows - 1, 0) - 2.0 * full
            flux = flux + other_flats[1 - k][h]
            total.append(full)
            flat.append(line)
            rest.append(
                DIFFUSE * flux + (GROWTH * (line - cube(own[0]) - cube(own[1])) + inner[k, 2, h])
            )
        totals.append(jnp.concatenate(total, axis=1))
        rests.append(jnp.concatenate(rest, axis=1))
        flats.append(jnp.concatenate(flat, axis=1))
    wide = times(jnp.concatenate(totals + flats, axis=0), pairs[...])
    tall = times(jnp.concatenate(rests, axis=0), pairs[:, : halves * LANES // 2])
    rows, lanes = tall.shape[0] // 2, tall.shape[1]
    means_two = [0.125 * wide[k * rows : (k + 1) * rows, :lanes] for k in range(2)]
    edges_two = [wide[k * rows : (k + 1) * rows, :lanes] for k in (2, 3)]
    forces_two = [
        0.125
        * (tall[k * rows : (k + 1) * rows] + DIFFUSE * wide[k * rows : (k + 1) * rows, lanes:])
        for k in range(2)
    ]
    half = planes // 2
    zero = [coarse_zero[0, p] for p in range(half)]
    mean_one = [coarse_one[0, p] for p in range(half)]
    force_zero = coarse_force(zero)
    force_one = coarse_force(mean_one)
    sweep_zero, sweep_one = [], []
    for p in range(half):
        parts = (coarse_zero[1, p], coarse_one[1, p], forces_two[p])
        sweep_zero.append(combine(WEIGHTS[0], parts))
        sweep_one.append(combine(WEIGHTS[1], parts))
    sends = []
    for e, p in enumerate((0, half - 1)):
        parts = (coarse_zero[2, e], coarse_one[2, e], edges_two[e])
        partial = sweep_zero[p] - mean_one[p] + (1.0 - later) * zero[p] - (0.5 * later) * force_zero[p]
        sends.append((
            (DIFFUSE / 8.0) * combine(WEIGHTS[0], parts) - (0.5 * COARSE * later) * zero[p],
            (DIFFUSE / 8.0) * combine(WEIGHTS[1], parts) + (0.5 * COARSE) * partial,
        ))
    for k in range(2):
        send_near[k], send_far[k] = low_high(sends[0][k], sends[1][k])
    for p in range(half):
        work[0, p] = zero[p]
        work[1, p] = mean_one[p]
        work[2, p] = means_two[p]
        work[3, p] = sweep_zero[p] - 0.5 * force_zero[p]
        work[4, p] = sweep_one[p] - 0.5 * force_one[p]
        two[planes, 0, p] = means_two[p]


def low_high(near, far):
    odd = lax.rem(lax.axis_index("space"), 2)
    return jnp.where(odd == 1, near, far), jnp.where(odd == 1, far, near)


def sides(near, far):
    pairs = [low_high(near[k], far[k]) for k in range(2)]
    return [v[0] for v in pairs], [v[1] for v in pairs]


def with_halo(work, low, high, own_low, own_high):
    half = work.shape[1]
    one = [work[3, p] for p in range(half)]
    two = [work[4, p] for p in range(half)]
    for p, got, own in ((0, low, own_low), (half - 1, high, own_high)):
        one[p] = one[p] + got[0]
        two[p] = two[p] + got[1] + (0.5 * COARSE) * own[0]
    return one, two


def coarse_steps(first, sweep_one, sweep_two):
    half = len(first)
    force = coarse_force(first)
    one = [first[p] + 0.5 * force[p] + sweep_one[p] for p in range(half)]
    force = coarse_force(one)
    return [one[p] + 0.5 * force[p] + sweep_two[p] for p in range(half)]


def fourth_kernel(work, near, far, own_near, own_far, end, send_near, send_far, swept):
    half = work.shape[1]
    low, high = sides(near, far)
    own_low, own_high = sides(own_near, own_far)
    for k, parts in enumerate(with_halo(work, low, high, own_low, own_high)):
        for p in range(half):
            swept[k, p] = parts[p]

    @pl.when(lax.axis_index("tm") == 0)
    def _():
        first = [work[0, p] for p in range(half)]
        two = coarse_steps(first, *[[swept[k, p] for p in range(half)] for k in range(2)])
        force = coarse_force(two)
        for p in range(half):
            end[p] = two[p]
        send_near[0], send_far[0] = low_high(two[0], two[half - 1])
        send_near[1], send_far[1] = low_high(
            two[0] + 0.5 * force[0], two[half - 1] + 0.5 * force[half - 1]
        )


class Planes:
    def __init__(self, spread, updated, parts, result, sem):
        self.updated, self.parts, self.result, self.sem = updated, parts, result, sem
        self.rows = parts.shape[2] // 2
        self.halves = parts.shape[1]
        self.spread = spread[...]
        self.copies = []

    def put(self, node, top, change, base):
        wide = times(change, self.spread)
        for p in (2 * top, 2 * top + 1):
            slot = len(self.copies)
            for h in range(self.halves):
                lanes = slice(h * LANES, (h + 1) * LANES)
                for q in range(2):
                    self.parts[slot, h, pl.ds(q, self.rows, stride=2), :] = (
                        base(p, h, q) + wide[:, lanes]
                    )
                self.result[slot, :, lanes] = self.parts[slot, h]
            copy = pltpu.make_async_copy(
                self.result.at[slot], self.updated.at[0, node, p], self.sem.at[slot]
            )
            copy.start()
            self.copies.append(copy)

    def finish(self):
        for copy in self.copies:
            copy.wait()


def last_kernel(
    nodes, ring_far, ring_near, end, one, two, moved, work, swept, spread,
    updated, held, parts, result, load_sem, sem,
):
    planes, halves = one.shape[0], one.shape[1]
    rows = one.shape[3]
    half = planes // 2
    section = lax.axis_index("tm")
    loads = [
        pltpu.make_async_copy(
            nodes.at[0, 0, :, :, pl.ds(h * LANES, LANES)], held.at[:, h], load_sem.at[h]
        )
        for h in range(halves)
    ]


    @pl.when(section == 0)
    def _():
        for copy in loads:
            copy.start()
        for copy in loads:
            copy.wait()

    def start(p, h, q):
        return jnp.where(section == 0, held[p, h, pl.ds(q, rows, stride=2), :], moved[p, h, q])

    out = Planes(spread, updated, parts, result, sem)
    first = [jnp.where(section == 0, work[0, p], end[p]) for p in range(half)]
    for top in range(half):
        mean = jnp.where(section == 0, work[0, top], moved[planes, 0, top])
        out.put(0, top, first[top] - mean, start)
    ring_low, ring_high = sides(ring_near, ring_far)
    scale = 0.5 * COARSE
    force = coarse_force(first)
    coarse_one = [first[p] + 0.5 * force[p] + swept[0, p] for p in range(half)]
    for p, v in ((0, ring_low), (half - 1, ring_high)):
        coarse_one[p] = coarse_one[p] + jnp.where(section == 0, 0.0, scale * v[0])
    for top in range(half):
        out.put(1, top, coarse_one[top] - work[1, top], lambda p, h, q: one[p, h, q])
    force = coarse_force(coarse_one)
    coarse_two = [coarse_one[p] + 0.5 * force[p] + swept[1, p] for p in range(half)]
    for p, v in ((0, ring_low), (half - 1, ring_high)):
        bend = jnp.where(section == 0, 0.0, v[1] + scale * first[p])
        coarse_two[p] = coarse_two[p] + scale * bend
    for top in range(half):
        out.put(2, top, coarse_two[top] - work[2, top], lambda p, h, q: two[p, h, q])
    out.finish()


def call(kernel, name, inputs, any_inputs, outs, scratch=(), any_outs=(), limit=VMEM_LIMIT,
         aliases=None, flops=0, size=0):
    def spec(far):
        return pl.BlockSpec(memory_space=pl.ANY if far else pltpu.VMEM)

    return pl.pallas_call(
        kernel,
        name=name,
        out_shape=[jax.ShapeDtypeStruct(s, F32) for s in outs],
        in_specs=[spec(k in any_inputs) for k in range(len(inputs))],
        out_specs=[spec(k in any_outs) for k in range(len(outs))],
        scratch_shapes=list(scratch),
        input_output_aliases=aliases or {},
        compiler_params=pltpu.CompilerParams(vmem_limit_bytes=limit),
        cost_estimate=pl.CostEstimate(flops=flops, bytes_accessed=size, transcendentals=0),
    )(*inputs)


def pairings(peers):
    near = [i ^ 1 for i in range(peers)]
    far = [(i + 1) % peers if i % 2 else (i - 1) % peers for i in range(peers)]
    return near, far


def exchange(near, far):
    to_near, to_far = pairings(lax.axis_size("space"))
    return (
        lax.ppermute(near, "space", list(enumerate(to_near))),
        lax.ppermute(far, "space", list(enumerate(to_far))),
    )


def swapped(value):
    return lax.ppermute(value, "tm", [(0, 1), (1, 0)])


def handed_on(near, far):
    peers = lax.axis_size("space")
    out = []
    for value, to in zip((far, near), pairings(peers)[::-1]):
        perm = [(i, peers + to[i]) for i in range(peers)] + [(peers + i, i) for i in range(peers)]
        out.append(lax.ppermute(value, ("tm", "space"), perm))
    return out


def local(nodes):
    _, _, planes, ny, nz = nodes.shape
    halves, rows, half = nz // LANES, ny // 2, planes // 2
    plane = (halves, 2, rows, LANES)
    field = (planes,) + plane
    quarter = (rows, nz // 2)
    pair = (2,) + quarter
    packed = (3, half) + quarter
    size = planes * ny * nz * 4

    pairs, spread = pair_matrix(nz), spread_matrix(nz // 2)
    a_near, a_far = call(
        edge_kernel, "edge_mix", (nodes,), (0,), [plane, plane],
        [
            pltpu.VMEM((2, 3, ny, nz), F32),
            pltpu.VMEM((2, halves, ny, LANES), F32),
            pltpu.SemaphoreType.DMA((2, 3)),
        ],
        limit=EDGE_LIMIT, size=size * 2, flops=size,
    )
    got_a_near, got_a_far = exchange(a_near, a_far)
    one_part, slope, rest, b_near, b_far, coarse_zero = call(
        first_kernel, "first_stage", (nodes, pairs), (), [field, field, field, plane, plane, packed],
        [pltpu.VMEM((5, ny, LANES), F32), pltpu.VMEM(field, F32), pltpu.VMEM(field, F32)],
        limit=FIRST_LIMIT,
        size=size * 6, flops=size * 10,
    )
    got_b_near, got_b_far = exchange(b_near, b_far)
    one, two_part, coarse_mid, inner = call(
        second_kernel, "second_stage",
        (one_part, slope, rest, got_a_near, got_a_far, a_near, a_far, pairs), (),
        [field, (planes + 1,) + plane, packed, (2, 3, halves, rows, LANES)],
        [pltpu.VMEM(field, F32)],
        size=size * 6, flops=size * 10,
    )
    two, h_near, h_far, work = call(
        third_kernel, "third_stage",
        (two_part, got_b_near, got_b_far, inner, coarse_zero, coarse_mid, pairs), (),
        [(planes + 1,) + plane, pair, pair, (5, half) + quarter], [pltpu.VMEM((2,) + plane, F32)],
        aliases={0: 0}, size=size * 3, flops=size * 5,
    )
    moved = swapped(two)
    got_near, got_far = exchange(h_near, h_far)
    end, f_near, f_far, swept = call(
        fourth_kernel, "coarse_chain", (work, got_near, got_far, h_near, h_far), (),
        [(half,) + quarter, pair, pair, (2, half) + quarter], size=size, flops=size,
    )
    ring_far, ring_near = handed_on(f_near, f_far)
    end = swapped(end)
    updated, = call(
        last_kernel, "update",
        (nodes, ring_far, ring_near, end, one, two, moved, work, swept, spread), (0,),
        [(1, 3, planes, ny, nz)],
        [
            pltpu.VMEM((planes, halves, ny, LANES), F32),
            pltpu.VMEM((3 * planes, halves, ny, LANES), F32),
            pltpu.VMEM((3 * planes, ny, nz), F32),
            pltpu.SemaphoreType.DMA((halves,)),
            pltpu.SemaphoreType.DMA((3 * planes,)),
        ],
        any_outs=(0,), size=size * 6, flops=size * 5,
    )
    return updated


def solution(mesh):
    in_specs = (P(("groups", "tm"), None, "space", None, None),)
    out_specs = P(("groups", "tm"), None, "space", None, None)
    return jax.shard_map(local, mesh=mesh, in_specs=in_specs, out_specs=out_specs, check_vma=False)
```

```python
import jax
import jax.numpy as jnp
import numpy as np
from jax import lax
from jax.experimental import pallas as pl
from jax.experimental.pallas import tpu as pltpu
from jax.sharding import PartitionSpec as P

DIFFUSE = 0.12
COARSE = DIFFUSE / 4.0
GROWTH = 0.5
WEIGHTS = ((5.0 / 24.0, 1.0 / 3.0, -1.0 / 24.0), (-1.0 / 24.0, 1.0 / 3.0, 5.0 / 24.0))
SECOND = (WEIGHTS[1][0], WEIGHTS[1][1] - 0.5, WEIGHTS[1][2])
LANES = 128
F32 = jnp.float32
BF16 = jnp.bfloat16
VMEM_LIMIT = 32 * 1024 * 1024
EDGE_LIMIT = 52 * 1024 * 1024
FIRST_LIMIT = 48 * 1024 * 1024


def combine(weights, parts):
    return weights[0] * parts[0] + weights[1] * parts[1] + weights[2] * parts[2]


def cube(v):
    return v * v * v


def z_neighbours(halves):
    count = len(halves)
    lane = lax.broadcasted_iota(jnp.int32, halves[0].shape, 1)
    fwd = [pltpu.roll(v, 1, 1) for v in halves]
    back = [pltpu.roll(v, LANES - 1, 1) for v in halves]
    out = []
    for k in range(count):
        before = jnp.where(lane == 0, fwd[(k - 1) % count], fwd[k])
        after = jnp.where(lane == LANES - 1, back[(k + 1) % count], back[k])
        out.append(before + after)
    return out


def y_neighbours(other, parity):
    rows = other.shape[0]
    return other + pltpu.roll(other, 1 if parity == 0 else rows - 1, 0)


def laplace_planes(ref, plane, planes, halves):
    for parity in range(2):
        own = [ref[plane, h, parity] for h in range(halves)]
        side = z_neighbours(own)
        for h in range(halves):
            total = side[h] + y_neighbours(ref[plane, h, 1 - parity], parity) - 6.0 * own[h]
            if plane > 0:
                total = total + ref[plane - 1, h, parity]
            if plane < planes - 1:
                total = total + ref[plane + 1, h, parity]
            yield h, parity, own[h], total


def coarse_force(field):
    planes = len(field)
    out = []
    for p in range(planes):
        v = field[p]
        rows, lanes = v.shape
        total = pltpu.roll(v, 1, 0) + pltpu.roll(v, rows - 1, 0)
        total = total + pltpu.roll(v, 1, 1) + pltpu.roll(v, lanes - 1, 1) - 6.0 * v
        if p > 0:
            total = total + field[p - 1]
        if p < planes - 1:
            total = total + field[p + 1]
        out.append(COARSE * total + GROWTH * (v - cube(v)))
    return out


def split(v):
    high = v.astype(BF16)
    low = (v - high.astype(F32)).astype(BF16)
    return high, low


def pair_matrix(size):
    out = np.zeros((size, size), np.float32)
    for k in range(size // 2):
        for offset in (0, 1):
            out[2 * k + offset, k] = 1.0
            out[2 * k + offset, size // 2 + k] = -1.0
        for offset in (-1, 2):
            out[(2 * k + offset) % size, size // 2 + k] = 1.0
    return jnp.asarray(out, BF16)


def spread_matrix(size):
    return jnp.asarray(np.repeat(np.eye(size, dtype=np.float32), 2, axis=1), BF16)


def times(v, matrix):
    high, low = split(v)
    return jnp.dot(high, matrix, preferred_element_type=F32) + jnp.dot(
        low, matrix, preferred_element_type=F32
    )


def restrict_field(ref, pairs, planes, halves):
    sums, bends = pairs[:, : halves * LANES // 2], pairs[:, halves * LANES // 2 :]

    def y_sum(p):
        return [ref[p, h, 0] + ref[p, h, 1] for h in range(halves)]

    means, forces = [], []
    flat = [y_sum(p) for p in range(planes)]
    for top in range(0, planes, 2):
        total, rest = [], []
        for h in range(halves):
            even = ref[top, h, 0] + ref[top + 1, h, 0]
            odd = ref[top, h, 1] + ref[top + 1, h, 1]
            both = even + odd
            rows = both.shape[0]
            flux = pltpu.roll(odd, 1, 0) + pltpu.roll(even, rows - 1, 0) - 2.0 * both
            if top > 0:
                flux = flux + flat[top - 1][h]
            if top + 2 < planes:
                flux = flux + flat[top + 2][h]
            cubes = cube(ref[top, h, 0]) + cube(ref[top + 1, h, 0])
            cubes = cubes + cube(ref[top, h, 1]) + cube(ref[top + 1, h, 1])
            total.append(both)
            rest.append(DIFFUSE * flux + GROWTH * (both - cubes))
        total = jnp.concatenate(total, axis=1)
        rest = jnp.concatenate(rest, axis=1)
        means.append(times(total, sums) * 0.125)
        forces.append((times(rest, sums) + DIFFUSE * times(total, bends)) * 0.125)
    edges = [times(jnp.concatenate(flat[p], axis=1), sums) for p in (0, planes - 1)]
    return means, forces, edges


def store_coarse(out, means, forces, edges):
    for k, parts in enumerate((means, forces, edges)):
        for p, v in enumerate(parts):
            out[k, p] = v


def outer_planes(planes):
    odd = lax.rem(lax.axis_index("space"), 2)
    return (1 - odd) * (planes - 1), odd * (planes - 1)


def edge_kernel(nodes, near, far, held, work, sem):
    planes, halves = nodes.shape[2], near.shape[0]
    rows = near.shape[2]
    copies = [
        [
            pltpu.make_async_copy(nodes.at[0, m, p], held.at[e, m], sem.at[e, m])
            for m in range(3)
        ]
        for e, p in enumerate(outer_planes(planes))
    ]
    for group in copies:
        for copy in group:
            copy.start()
    for e, out in enumerate((near, far)):
        for copy in copies[e]:
            copy.wait()
        for h in range(halves):
            lanes = pl.ds(h * LANES, LANES)
            work[e, h] = combine(WEIGHTS[0], [held[e, m, :, lanes] for m in range(3)])
            for q in range(2):
                out[h, q] = work[e, h, pl.ds(q, rows, stride=2), :]


def first_kernel(nodes, pairs, one, slope, rest, near, far, coarse, work, start, mix):
    planes, halves = one.shape[0], one.shape[1]
    rows = one.shape[3]
    for p in range(planes):
        for h in range(halves):
            lanes = pl.ds(h * LANES, LANES)
            parts = [nodes[0, m, p, :, lanes] for m in range(3)]
            cubes = [cube(v) for v in parts]
            a = combine(WEIGHTS[0], parts)
            d = combine(SECOND, parts)
            work[0] = parts[0]
            work[1] = a
            work[2] = d
            work[3] = parts[0] + GROWTH * (a - combine(WEIGHTS[0], cubes))
            work[4] = GROWTH * (d - combine(SECOND, cubes))
            for q in range(2):
                for k, out in enumerate((start, mix, slope, one, rest)):
                    out[p, h, q] = work[k, pl.ds(q, rows, stride=2), :]
    for p in range(planes):
        for h, q, _, laplace in laplace_planes(mix, p, planes, halves):
            one[p, h, q] = one[p, h, q] + DIFFUSE * laplace
    for p, out in zip(outer_planes(planes), (near, far)):
        out[...] = 0.5 * one[p] + slope[p]
    store_coarse(coarse, *restrict_field(start, pairs, planes, halves))


def second_kernel(
    one_in, slope, rest, near, far, own_near, own_far, pairs, coarse_zero, one, two, coarse, inner, coarse_forces, mix
):
    planes, halves = one_in.shape[0], one_in.shape[1]
    outer = outer_planes(planes)
    for p in range(1, planes - 1):
        one[p] = one_in[p]
    for p, halo in zip(outer, (near, far)):
        one[p] = one_in[p] + DIFFUSE * halo[...]
    for p in range(planes):
        mix[p] = 0.5 * one[p] + slope[p]
    for p in range(planes):
        for h, q, _, laplace in laplace_planes(mix, p, planes, halves):
            value = one[p, h, q]
            two[p, h, q] = (
                value + DIFFUSE * laplace + (0.5 * GROWTH) * (value - cube(value)) + rest[p, h, q]
            )
    for p, own in zip(outer, (own_near, own_far)):
        two[p] = two[p] + (0.5 * DIFFUSE * DIFFUSE) * own[...]
    for k, p in enumerate((1, planes - 2)):
        for h in range(halves):
            even, odd = two[p, h, 0], two[p, h, 1]
            inner[k, 0, h] = even
            inner[k, 1, h] = odd
            inner[k, 2, h] = GROWTH * (even + odd - cube(even) - cube(odd))
    means, forces, edges = restrict_field(one, pairs, planes, halves)
    store_coarse(coarse, means, forces, edges)
    for k, field in enumerate(([coarse_zero[0, p] for p in range(planes // 2)], means)):
        for p, v in enumerate(coarse_force(field)):
            coarse_forces[k, p] = v


def third_kernel(
    two_in, near, far, inner, coarse_zero, coarse_one, coarse_forces, pairs, two, send_near, send_far, work, outer
):
    planes, halves = two_in.shape[0] - 1, two_in.shape[1]
    later = lax.axis_index("tm").astype(F32)
    for p, halo in zip(outer_planes(planes), (near, far)):
        outer[p // (planes - 1)] = two_in[p] + DIFFUSE * halo[...]
    totals, rests, flats = [], [], []
    other_flats = [[inner[k, 0, h] + inner[k, 1, h] for h in range(halves)] for k in range(2)]
    for k in range(2):
        two[k * (planes - 1)] = outer[k]
        total, rest, flat = [], [], []
        for h in range(halves):
            own = outer[k, h, 0], outer[k, h, 1]
            even, odd = own[0] + inner[k, 0, h], own[1] + inner[k, 1, h]
            line = own[0] + own[1]
            full = line + other_flats[k][h]
            rows = full.shape[0]
            flux = pltpu.roll(odd, 1, 0) + pltpu.roll(even, rows - 1, 0) - 2.0 * full
            flux = flux + other_flats[1 - k][h]
            total.append(full)
            flat.append(line)
            rest.append(
                DIFFUSE * flux + (GROWTH * (line - cube(own[0]) - cube(own[1])) + inner[k, 2, h])
            )
        totals.append(jnp.concatenate(total, axis=1))
        rests.append(jnp.concatenate(rest, axis=1))
        flats.append(jnp.concatenate(flat, axis=1))
    wide = times(jnp.concatenate(totals + flats, axis=0), pairs[...])
    tall = times(jnp.concatenate(rests, axis=0), pairs[:, : halves * LANES // 2])
    rows, lanes = tall.shape[0] // 2, tall.shape[1]
    means_two = [0.125 * wide[k * rows : (k + 1) * rows, :lanes] for k in range(2)]
    edges_two = [wide[k * rows : (k + 1) * rows, :lanes] for k in (2, 3)]
    forces_two = [
        0.125
        * (tall[k * rows : (k + 1) * rows] + DIFFUSE * wide[k * rows : (k + 1) * rows, lanes:])
        for k in range(2)
    ]
    half = planes // 2
    zero = [coarse_zero[0, p] for p in range(half)]
    mean_one = [coarse_one[0, p] for p in range(half)]
    force_zero = [coarse_forces[0, p] for p in range(half)]
    force_one = [coarse_forces[1, p] for p in range(half)]
    sweep_zero, sweep_one = [], []
    for p in range(half):
        parts = (coarse_zero[1, p], coarse_one[1, p], forces_two[p])
        sweep_zero.append(combine(WEIGHTS[0], parts))
        sweep_one.append(combine(WEIGHTS[1], parts))
    sends = []
    for e, p in enumerate((0, half - 1)):
        parts = (coarse_zero[2, e], coarse_one[2, e], edges_two[e])
        partial = sweep_zero[p] - mean_one[p] + (1.0 - later) * zero[p] - (0.5 * later) * force_zero[p]
        sends.append((
            (DIFFUSE / 8.0) * combine(WEIGHTS[0], parts) - (0.5 * COARSE * later) * zero[p],
            (DIFFUSE / 8.0) * combine(WEIGHTS[1], parts) + (0.5 * COARSE) * partial,
        ))
    for k in range(2):
        send_near[k], send_far[k] = low_high(sends[0][k], sends[1][k])
    for p in range(half):
        work[0, p] = zero[p]
        work[1, p] = mean_one[p]
        work[2, p] = means_two[p]
        work[3, p] = sweep_zero[p] - 0.5 * force_zero[p]
        work[4, p] = sweep_one[p] - 0.5 * force_one[p]
        two[planes, 0, p] = means_two[p]


def low_high(near, far):
    odd = lax.rem(lax.axis_index("space"), 2)
    return jnp.where(odd == 1, near, far), jnp.where(odd == 1, far, near)


def sides(near, far):
    pairs = [low_high(near[k], far[k]) for k in range(2)]
    return [v[0] for v in pairs], [v[1] for v in pairs]


def with_halo(work, low, high, own_low, own_high):
    half = work.shape[1]
    one = [work[3, p] for p in range(half)]
    two = [work[4, p] for p in range(half)]
    for p, got, own in ((0, low, own_low), (half - 1, high, own_high)):
        one[p] = one[p] + got[0]
        two[p] = two[p] + got[1] + (0.5 * COARSE) * own[0]
    return one, two


def coarse_steps(first, force, sweep_one, sweep_two):
    half = len(first)
    one = [first[p] + 0.5 * force[p] + sweep_one[p] for p in range(half)]
    force = coarse_force(one)
    return [one[p] + 0.5 * force[p] + sweep_two[p] for p in range(half)]


def fourth_kernel(work, near, far, own_near, own_far, coarse_forces, end, send_near, send_far, swept):
    half = work.shape[1]
    low, high = sides(near, far)
    own_low, own_high = sides(own_near, own_far)
    for k, parts in enumerate(with_halo(work, low, high, own_low, own_high)):
        for p in range(half):
            swept[k, p] = parts[p]

    @pl.when(lax.axis_index("tm") == 0)
    def _():
        first = [work[0, p] for p in range(half)]
        start = [coarse_forces[0, p] for p in range(half)]
        two = coarse_steps(first, start, *[[swept[k, p] for p in range(half)] for k in range(2)])
        force = coarse_force(two)
        for p in range(half):
            end[p] = two[p]
        send_near[0], send_far[0] = low_high(two[0], two[half - 1])
        send_near[1], send_far[1] = low_high(
            two[0] + 0.5 * force[0], two[half - 1] + 0.5 * force[half - 1]
        )


class Planes:
    def __init__(self, spread, updated, parts, result, sem):
        self.updated, self.parts, self.result, self.sem = updated, parts, result, sem
        self.rows = parts.shape[2] // 2
        self.halves = parts.shape[1]
        self.spread = spread[...]
        self.copies = []

    def put(self, node, top, change, base):
        wide = times(change, self.spread)
        for p in (2 * top, 2 * top + 1):
            slot = len(self.copies)
            for h in range(self.halves):
                lanes = slice(h * LANES, (h + 1) * LANES)
                for q in range(2):
                    self.parts[slot, h, pl.ds(q, self.rows, stride=2), :] = (
                        base(p, h, q) + wide[:, lanes]
                    )
                self.result[slot, :, lanes] = self.parts[slot, h]
            copy = pltpu.make_async_copy(
                self.result.at[slot], self.updated.at[0, node, p], self.sem.at[slot]
            )
            copy.start()
            self.copies.append(copy)

    def finish(self):
        for copy in self.copies:
            copy.wait()


def last_kernel(
    nodes, ring_far, ring_near, end, one, two, moved, work, swept, spread,
    updated, held, parts, result, load_sem, sem,
):
    planes, halves = one.shape[0], one.shape[1]
    rows = one.shape[3]
    half = planes // 2
    section = lax.axis_index("tm")
    loads = [
        pltpu.make_async_copy(
            nodes.at[0, 0, :, :, pl.ds(h * LANES, LANES)], held.at[:, h], load_sem.at[h]
        )
        for h in range(halves)
    ]


    @pl.when(section == 0)
    def _():
        for copy in loads:
            copy.start()
        for copy in loads:
            copy.wait()

    def start(p, h, q):
        return jnp.where(section == 0, held[p, h, pl.ds(q, rows, stride=2), :], moved[p, h, q])

    out = Planes(spread, updated, parts, result, sem)
    first = [jnp.where(section == 0, work[0, p], end[p]) for p in range(half)]
    for top in range(half):
        mean = jnp.where(section == 0, work[0, top], moved[planes, 0, top])
        out.put(0, top, first[top] - mean, start)
    ring_low, ring_high = sides(ring_near, ring_far)
    scale = 0.5 * COARSE
    force = coarse_force(first)
    coarse_one = [first[p] + 0.5 * force[p] + swept[0, p] for p in range(half)]
    for p, v in ((0, ring_low), (half - 1, ring_high)):
        coarse_one[p] = coarse_one[p] + jnp.where(section == 0, 0.0, scale * v[0])
    for top in range(half):
        out.put(1, top, coarse_one[top] - work[1, top], lambda p, h, q: one[p, h, q])
    force = coarse_force(coarse_one)
    coarse_two = [coarse_one[p] + 0.5 * force[p] + swept[1, p] for p in range(half)]
    for p, v in ((0, ring_low), (half - 1, ring_high)):
        bend = jnp.where(section == 0, 0.0, v[1] + scale * first[p])
        coarse_two[p] = coarse_two[p] + scale * bend
    for top in range(half):
        out.put(2, top, coarse_two[top] - work[2, top], lambda p, h, q: two[p, h, q])
    out.finish()


def call(kernel, name, inputs, any_inputs, outs, scratch=(), any_outs=(), limit=VMEM_LIMIT,
         aliases=None, flops=0, size=0):
    def spec(far):
        return pl.BlockSpec(memory_space=pl.ANY if far else pltpu.VMEM)

    return pl.pallas_call(
        kernel,
        name=name,
        out_shape=[jax.ShapeDtypeStruct(s, F32) for s in outs],
        in_specs=[spec(k in any_inputs) for k in range(len(inputs))],
        out_specs=[spec(k in any_outs) for k in range(len(outs))],
        scratch_shapes=list(scratch),
        input_output_aliases=aliases or {},
        compiler_params=pltpu.CompilerParams(vmem_limit_bytes=limit),
        cost_estimate=pl.CostEstimate(flops=flops, bytes_accessed=size, transcendentals=0),
    )(*inputs)


def pairings(peers):
    near = [i ^ 1 for i in range(peers)]
    far = [(i + 1) % peers if i % 2 else (i - 1) % peers for i in range(peers)]
    return near, far


def exchange(near, far):
    to_near, to_far = pairings(lax.axis_size("space"))
    return (
        lax.ppermute(near, "space", list(enumerate(to_near))),
        lax.ppermute(far, "space", list(enumerate(to_far))),
    )


def swapped(value):
    return lax.ppermute(value, "tm", [(0, 1), (1, 0)])


def handed_on(near, far):
    peers = lax.axis_size("space")
    out = []
    for value, to in zip((far, near), pairings(peers)[::-1]):
        perm = [(i, peers + to[i]) for i in range(peers)] + [(peers + i, i) for i in range(peers)]
        out.append(lax.ppermute(value, ("tm", "space"), perm))
    return out


def local(nodes):
    _, _, planes, ny, nz = nodes.shape
    halves, rows, half = nz // LANES, ny // 2, planes // 2
    plane = (halves, 2, rows, LANES)
    field = (planes,) + plane
    quarter = (rows, nz // 2)
    pair = (2,) + quarter
    packed = (3, half) + quarter
    size = planes * ny * nz * 4

    pairs, spread = pair_matrix(nz), spread_matrix(nz // 2)
    a_near, a_far = call(
        edge_kernel, "edge_mix", (nodes,), (0,), [plane, plane],
        [
            pltpu.VMEM((2, 3, ny, nz), F32),
            pltpu.VMEM((2, halves, ny, LANES), F32),
            pltpu.SemaphoreType.DMA((2, 3)),
        ],
        limit=EDGE_LIMIT, size=size * 2, flops=size,
    )
    got_a_near, got_a_far = exchange(a_near, a_far)
    one_part, slope, rest, b_near, b_far, coarse_zero = call(
        first_kernel, "first_stage", (nodes, pairs), (), [field, field, field, plane, plane, packed],
        [pltpu.VMEM((5, ny, LANES), F32), pltpu.VMEM(field, F32), pltpu.VMEM(field, F32)],
        limit=FIRST_LIMIT,
        size=size * 6, flops=size * 10,
    )
    got_b_near, got_b_far = exchange(b_near, b_far)
    one, two_part, coarse_mid, inner, coarse_forces = call(
        second_kernel, "second_stage",
        (one_part, slope, rest, got_a_near, got_a_far, a_near, a_far, pairs, coarse_zero), (),
        [field, (planes + 1,) + plane, packed, (2, 3, halves, rows, LANES), (2, half) + quarter],
        [pltpu.VMEM(field, F32)],
        size=size * 6, flops=size * 10,
    )
    two, h_near, h_far, work = call(
        third_kernel, "third_stage",
        (two_part, got_b_near, got_b_far, inner, coarse_zero, coarse_mid, coarse_forces, pairs), (),
        [(planes + 1,) + plane, pair, pair, (5, half) + quarter], [pltpu.VMEM((2,) + plane, F32)],
        aliases={0: 0}, size=size * 3, flops=size * 5,
    )
    moved = swapped(two)
    got_near, got_far = exchange(h_near, h_far)
    end, f_near, f_far, swept = call(
        fourth_kernel, "coarse_chain", (work, got_near, got_far, h_near, h_far, coarse_forces), (),
        [(half,) + quarter, pair, pair, (2, half) + quarter], size=size, flops=size,
    )
    ring_far, ring_near = handed_on(f_near, f_far)
    end = swapped(end)
    updated, = call(
        last_kernel, "update",
        (nodes, ring_far, ring_near, end, one, two, moved, work, swept, spread), (0,),
        [(1, 3, planes, ny, nz)],
        [
            pltpu.VMEM((planes, halves, ny, LANES), F32),
            pltpu.VMEM((3 * planes, halves, ny, LANES), F32),
            pltpu.VMEM((3 * planes, ny, nz), F32),
            pltpu.SemaphoreType.DMA((halves,)),
            pltpu.SemaphoreType.DMA((3 * planes,)),
        ],
        any_outs=(0,), size=size * 6, flops=size * 5,
    )
    return updated


def solution(mesh):
    in_specs = (P(("groups", "tm"), None, "space", None, None),)
    out_specs = P(("groups", "tm"), None, "space", None, None)
    return jax.shard_map(local, mesh=mesh, in_specs=in_specs, out_specs=out_specs, check_vma=False)
```

```python
import jax
import jax.numpy as jnp
import numpy as np
from jax import lax
from jax.experimental import pallas as pl
from jax.experimental.pallas import tpu as pltpu
from jax.sharding import PartitionSpec as P

DIFFUSE = 0.12
COARSE = DIFFUSE / 4.0
GROWTH = 0.5
WEIGHTS = ((5.0 / 24.0, 1.0 / 3.0, -1.0 / 24.0), (-1.0 / 24.0, 1.0 / 3.0, 5.0 / 24.0))
SECOND = (WEIGHTS[1][0], WEIGHTS[1][1] - 0.5, WEIGHTS[1][2])
LANES = 128
F32 = jnp.float32
BF16 = jnp.bfloat16
VMEM_LIMIT = 32 * 1024 * 1024
EDGE_LIMIT = 52 * 1024 * 1024
FIRST_LIMIT = 48 * 1024 * 1024


def combine(weights, parts):
    return weights[0] * parts[0] + weights[1] * parts[1] + weights[2] * parts[2]


def cube(v):
    return v * v * v


def z_neighbours(halves):
    count = len(halves)
    lane = lax.broadcasted_iota(jnp.int32, halves[0].shape, 1)
    fwd = [pltpu.roll(v, 1, 1) for v in halves]
    back = [pltpu.roll(v, LANES - 1, 1) for v in halves]
    out = []
    for k in range(count):
        before = jnp.where(lane == 0, fwd[(k - 1) % count], fwd[k])
        after = jnp.where(lane == LANES - 1, back[(k + 1) % count], back[k])
        out.append(before + after)
    return out


def y_neighbours(other, parity):
    rows = other.shape[0]
    return other + pltpu.roll(other, 1 if parity == 0 else rows - 1, 0)


def laplace_planes(ref, plane, planes, halves):
    for parity in range(2):
        own = [ref[plane, h, parity] for h in range(halves)]
        side = z_neighbours(own)
        for h in range(halves):
            total = side[h] + y_neighbours(ref[plane, h, 1 - parity], parity) - 6.0 * own[h]
            if plane > 0:
                total = total + ref[plane - 1, h, parity]
            if plane < planes - 1:
                total = total + ref[plane + 1, h, parity]
            yield h, parity, own[h], total


def coarse_force(field):
    planes = len(field)
    out = []
    for p in range(planes):
        v = field[p]
        rows, lanes = v.shape
        total = pltpu.roll(v, 1, 0) + pltpu.roll(v, rows - 1, 0)
        total = total + pltpu.roll(v, 1, 1) + pltpu.roll(v, lanes - 1, 1) - 6.0 * v
        if p > 0:
            total = total + field[p - 1]
        if p < planes - 1:
            total = total + field[p + 1]
        out.append(COARSE * total + GROWTH * (v - cube(v)))
    return out


def split(v):
    high = v.astype(BF16)
    low = (v - high.astype(F32)).astype(BF16)
    return high, low


def pair_matrix(size):
    out = np.zeros((size, size), np.float32)
    for k in range(size // 2):
        for offset in (0, 1):
            out[2 * k + offset, k] = 1.0
            out[2 * k + offset, size // 2 + k] = -1.0
        for offset in (-1, 2):
            out[(2 * k + offset) % size, size // 2 + k] = 1.0
    return jnp.asarray(out, BF16)


def spread_matrix(size):
    row = lax.broadcasted_iota(jnp.int32, (size, 2 * size), 0)
    col = lax.broadcasted_iota(jnp.int32, (size, 2 * size), 1)
    return jnp.where((col == 2 * row) | (col == 2 * row + 1), 1.0, 0.0).astype(F32).astype(BF16)


def times(v, matrix):
    high, low = split(v)
    return jnp.dot(high, matrix, preferred_element_type=F32) + jnp.dot(
        low, matrix, preferred_element_type=F32
    )


def restrict_field(ref, pairs, planes, halves):
    sums, bends = pairs[:, : halves * LANES // 2], pairs[:, halves * LANES // 2 :]

    def y_sum(p):
        return [ref[p, h, 0] + ref[p, h, 1] for h in range(halves)]

    means, forces = [], []
    flat = [y_sum(p) for p in range(planes)]
    for top in range(0, planes, 2):
        total, rest = [], []
        for h in range(halves):
            even = ref[top, h, 0] + ref[top + 1, h, 0]
            odd = ref[top, h, 1] + ref[top + 1, h, 1]
            both = even + odd
            rows = both.shape[0]
            flux = pltpu.roll(odd, 1, 0) + pltpu.roll(even, rows - 1, 0) - 2.0 * both
            if top > 0:
                flux = flux + flat[top - 1][h]
            if top + 2 < planes:
                flux = flux + flat[top + 2][h]
            cubes = cube(ref[top, h, 0]) + cube(ref[top + 1, h, 0])
            cubes = cubes + cube(ref[top, h, 1]) + cube(ref[top + 1, h, 1])
            total.append(both)
            rest.append(DIFFUSE * flux + GROWTH * (both - cubes))
        total = jnp.concatenate(total, axis=1)
        rest = jnp.concatenate(rest, axis=1)
        means.append(times(total, sums) * 0.125)
        forces.append((times(rest, sums) + DIFFUSE * times(total, bends)) * 0.125)
    edges = [times(jnp.concatenate(flat[p], axis=1), sums) for p in (0, planes - 1)]
    return means, forces, edges


def store_coarse(out, means, forces, edges):
    for k, parts in enumerate((means, forces, edges)):
        for p, v in enumerate(parts):
            out[k, p] = v


def outer_planes(planes):
    odd = lax.rem(lax.axis_index("space"), 2)
    return (1 - odd) * (planes - 1), odd * (planes - 1)


def edge_kernel(nodes, near, far, held, work, sem):
    planes, halves = nodes.shape[2], near.shape[0]
    rows = near.shape[2]
    copies = [
        [
            pltpu.make_async_copy(nodes.at[0, m, p], held.at[e, m], sem.at[e, m])
            for m in range(3)
        ]
        for e, p in enumerate(outer_planes(planes))
    ]
    for group in copies:
        for copy in group:
            copy.start()
    for e, out in enumerate((near, far)):
        for copy in copies[e]:
            copy.wait()
        for h in range(halves):
            lanes = pl.ds(h * LANES, LANES)
            work[e, h] = combine(WEIGHTS[0], [held[e, m, :, lanes] for m in range(3)])
            for q in range(2):
                out[h, q] = work[e, h, pl.ds(q, rows, stride=2), :]


def first_kernel(nodes, pairs, one, slope, rest, near, far, coarse, start, work, mix):
    planes, halves = one.shape[0], one.shape[1]
    rows = one.shape[3]
    for p in range(planes):
        for h in range(halves):
            lanes = pl.ds(h * LANES, LANES)
            parts = [nodes[0, m, p, :, lanes] for m in range(3)]
            cubes = [cube(v) for v in parts]
            a = combine(WEIGHTS[0], parts)
            d = combine(SECOND, parts)
            work[0] = parts[0]
            work[1] = a
            work[2] = d
            work[3] = parts[0] + GROWTH * (a - combine(WEIGHTS[0], cubes))
            work[4] = GROWTH * (d - combine(SECOND, cubes))
            for q in range(2):
                for k, out in enumerate((start, mix, slope, one, rest)):
                    out[p, h, q] = work[k, pl.ds(q, rows, stride=2), :]
    for p in range(planes):
        for h, q, _, laplace in laplace_planes(mix, p, planes, halves):
            one[p, h, q] = one[p, h, q] + DIFFUSE * laplace
    for p, out in zip(outer_planes(planes), (near, far)):
        out[...] = 0.5 * one[p] + slope[p]
    store_coarse(coarse, *restrict_field(start, pairs, planes, halves))


def second_kernel(
    one_in, slope, rest, near, far, own_near, own_far, pairs, coarse_zero, one, two, coarse, inner, coarse_forces, mix
):
    planes, halves = one_in.shape[0], one_in.shape[1]
    outer = outer_planes(planes)
    for p in range(1, planes - 1):
        one[p] = one_in[p]
    for p, halo in zip(outer, (near, far)):
        one[p] = one_in[p] + DIFFUSE * halo[...]
    for p in range(planes):
        mix[p] = 0.5 * one[p] + slope[p]
    for p in range(planes):
        for h, q, _, laplace in laplace_planes(mix, p, planes, halves):
            value = one[p, h, q]
            two[p, h, q] = (
                value + DIFFUSE * laplace + (0.5 * GROWTH) * (value - cube(value)) + rest[p, h, q]
            )
    for p, own in zip(outer, (own_near, own_far)):
        two[p] = two[p] + (0.5 * DIFFUSE * DIFFUSE) * own[...]
    for k, p in enumerate((1, planes - 2)):
        for h in range(halves):
            even, odd = two[p, h, 0], two[p, h, 1]
            inner[k, 0, h] = even
            inner[k, 1, h] = odd
            inner[k, 2, h] = GROWTH * (even + odd - cube(even) - cube(odd))
    means, forces, edges = restrict_field(one, pairs, planes, halves)
    store_coarse(coarse, means, forces, edges)
    for k, field in enumerate(([coarse_zero[0, p] for p in range(planes // 2)], means)):
        for p, v in enumerate(coarse_force(field)):
            coarse_forces[k, p] = v


def third_kernel(
    two_in, near, far, inner, coarse_zero, coarse_one, coarse_forces, pairs, two, send_near, send_far, work, outer
):
    planes, halves = two_in.shape[0] - 1, two_in.shape[1]
    later = lax.axis_index("tm").astype(F32)
    for p, halo in zip(outer_planes(planes), (near, far)):
        outer[p // (planes - 1)] = two_in[p] + DIFFUSE * halo[...]
    totals, rests, flats = [], [], []
    other_flats = [[inner[k, 0, h] + inner[k, 1, h] for h in range(halves)] for k in range(2)]
    for k in range(2):
        two[k * (planes - 1)] = outer[k]
        total, rest, flat = [], [], []
        for h in range(halves):
            own = outer[k, h, 0], outer[k, h, 1]
            even, odd = own[0] + inner[k, 0, h], own[1] + inner[k, 1, h]
            line = own[0] + own[1]
            full = line + other_flats[k][h]
            rows = full.shape[0]
            flux = pltpu.roll(odd, 1, 0) + pltpu.roll(even, rows - 1, 0) - 2.0 * full
            flux = flux + other_flats[1 - k][h]
            total.append(full)
            flat.append(line)
            rest.append(
                DIFFUSE * flux + (GROWTH * (line - cube(own[0]) - cube(own[1])) + inner[k, 2, h])
            )
        totals.append(jnp.concatenate(total, axis=1))
        rests.append(jnp.concatenate(rest, axis=1))
        flats.append(jnp.concatenate(flat, axis=1))
    wide = times(jnp.concatenate(totals + flats, axis=0), pairs[...])
    tall = times(jnp.concatenate(rests, axis=0), pairs[:, : halves * LANES // 2])
    rows, lanes = tall.shape[0] // 2, tall.shape[1]
    means_two = [0.125 * wide[k * rows : (k + 1) * rows, :lanes] for k in range(2)]
    edges_two = [wide[k * rows : (k + 1) * rows, :lanes] for k in (2, 3)]
    forces_two = [
        0.125
        * (tall[k * rows : (k + 1) * rows] + DIFFUSE * wide[k * rows : (k + 1) * rows, lanes:])
        for k in range(2)
    ]
    half = planes // 2
    zero = [coarse_zero[0, p] for p in range(half)]
    mean_one = [coarse_one[0, p] for p in range(half)]
    force_zero = [coarse_forces[0, p] for p in range(half)]
    force_one = [coarse_forces[1, p] for p in range(half)]
    sweep_zero, sweep_one = [], []
    for p in range(half):
        parts = (coarse_zero[1, p], coarse_one[1, p], forces_two[p])
        sweep_zero.append(combine(WEIGHTS[0], parts))
        sweep_one.append(combine(WEIGHTS[1], parts))
    sends = []
    for e, p in enumerate((0, half - 1)):
        parts = (coarse_zero[2, e], coarse_one[2, e], edges_two[e])
        partial = sweep_zero[p] - mean_one[p] + (1.0 - later) * zero[p] - (0.5 * later) * force_zero[p]
        sends.append((
            (DIFFUSE / 8.0) * combine(WEIGHTS[0], parts) - (0.5 * COARSE * later) * zero[p],
            (DIFFUSE / 8.0) * combine(WEIGHTS[1], parts) + (0.5 * COARSE) * partial,
        ))
    for k in range(2):
        send_near[k], send_far[k] = low_high(sends[0][k], sends[1][k])
    for p in range(half):
        work[0, p] = zero[p]
        work[1, p] = mean_one[p]
        work[2, p] = means_two[p]
        work[3, p] = sweep_zero[p] - 0.5 * force_zero[p]
        work[4, p] = sweep_one[p] - 0.5 * force_one[p]
        two[planes, 0, p] = means_two[p]


def low_high(near, far):
    odd = lax.rem(lax.axis_index("space"), 2)
    return jnp.where(odd == 1, near, far), jnp.where(odd == 1, far, near)


def sides(near, far):
    pairs = [low_high(near[k], far[k]) for k in range(2)]
    return [v[0] for v in pairs], [v[1] for v in pairs]


def with_halo(work, low, high, own_low, own_high):
    half = work.shape[1]
    one = [work[3, p] for p in range(half)]
    two = [work[4, p] for p in range(half)]
    for p, got, own in ((0, low, own_low), (half - 1, high, own_high)):
        one[p] = one[p] + got[0]
        two[p] = two[p] + got[1] + (0.5 * COARSE) * own[0]
    return one, two


def coarse_steps(first, force, sweep_one, sweep_two):
    half = len(first)
    one = [first[p] + 0.5 * force[p] + sweep_one[p] for p in range(half)]
    force = coarse_force(one)
    return [one[p] + 0.5 * force[p] + sweep_two[p] for p in range(half)]


def fourth_kernel(
    work, near, far, own_near, own_far, coarse_forces, held, end, send_near, send_far, swept, passed
):
    del held, passed
    half = work.shape[1]
    low, high = sides(near, far)
    own_low, own_high = sides(own_near, own_far)
    for k, parts in enumerate(with_halo(work, low, high, own_low, own_high)):
        for p in range(half):
            swept[k, p] = parts[p]

    @pl.when(lax.axis_index("tm") == 0)
    def _():
        first = [work[0, p] for p in range(half)]
        start = [coarse_forces[0, p] for p in range(half)]
        two = coarse_steps(first, start, *[[swept[k, p] for p in range(half)] for k in range(2)])
        force = coarse_force(two)
        for p in range(half):
            end[p] = two[p]
        send_near[0], send_far[0] = low_high(two[0], two[half - 1])
        send_near[1], send_far[1] = low_high(
            two[0] + 0.5 * force[0], two[half - 1] + 0.5 * force[half - 1]
        )


class Planes:
    def __init__(self, updated, parts, result, sem):
        self.updated, self.parts, self.result, self.sem = updated, parts, result, sem
        self.rows = parts.shape[2] // 2
        self.halves = parts.shape[1]
        self.spread = spread_matrix(LANES * self.halves // 2)
        self.copies = []

    def put(self, node, top, change, base):
        wide = times(change, self.spread)
        for p in (2 * top, 2 * top + 1):
            slot = len(self.copies)
            for h in range(self.halves):
                lanes = slice(h * LANES, (h + 1) * LANES)
                for q in range(2):
                    self.parts[slot, h, pl.ds(q, self.rows, stride=2), :] = (
                        base(p, h, q) + wide[:, lanes]
                    )
                self.result[slot, :, lanes] = self.parts[slot, h]
            copy = pltpu.make_async_copy(
                self.result.at[slot], self.updated.at[0, node, p], self.sem.at[slot]
            )
            copy.start()
            self.copies.append(copy)

    def finish(self):
        for copy in self.copies:
            copy.wait()


def step_kernel(ring_far, ring_near, end, work, swept, first, change):
    half = work.shape[1]
    section = lax.axis_index("tm")
    ring_low, ring_high = sides(ring_near, ring_far)
    scale = 0.5 * COARSE
    start = [jnp.where(section == 0, work[0, p], end[p]) for p in range(half)]
    force = coarse_force(start)
    one = [start[p] + 0.5 * force[p] + swept[0, p] for p in range(half)]
    for p, v in ((0, ring_low), (half - 1, ring_high)):
        one[p] = one[p] + jnp.where(section == 0, 0.0, scale * v[0])
    force = coarse_force(one)
    two = [one[p] + 0.5 * force[p] + swept[1, p] for p in range(half)]
    for p, v in ((0, ring_low), (half - 1, ring_high)):
        two[p] = two[p] + scale * jnp.where(section == 0, 0.0, v[1] + scale * start[p])
    for p in range(half):
        first[p] = start[p]
        change[0, p] = one[p] - work[1, p]
        change[1, p] = two[p] - work[2, p]


def last_kernel(
    own, first, change, moved, one, two, work, updated, parts, result, sem
):
    planes, half = one.shape[0], one.shape[0] // 2
    section = lax.axis_index("tm")
    out = Planes(updated, parts, result, sem)
    for top in range(half):
        out.put(1, top, change[0, top], lambda p, h, q: one[p, h, q])
    for top in range(half):
        out.put(2, top, change[1, top], lambda p, h, q: two[p, h, q])

    def start(p, h, q):
        return jnp.where(section == 0, own[p, h, q], moved[p, h, q])

    for top in range(half):
        mean = jnp.where(section == 0, work[0, top], moved[planes, 0, top])
        out.put(0, top, first[top] - mean, start)
    out.finish()


def call(kernel, name, inputs, any_inputs, outs, scratch=(), any_outs=(), limit=VMEM_LIMIT,
         aliases=None, flops=0, size=0):
    def spec(far):
        return pl.BlockSpec(memory_space=pl.ANY if far else pltpu.VMEM)

    return pl.pallas_call(
        kernel,
        name=name,
        out_shape=[jax.ShapeDtypeStruct(s, F32) for s in outs],
        in_specs=[spec(k in any_inputs) for k in range(len(inputs))],
        out_specs=[spec(k in any_outs) for k in range(len(outs))],
        scratch_shapes=list(scratch),
        input_output_aliases=aliases or {},
        compiler_params=pltpu.CompilerParams(vmem_limit_bytes=limit),
        cost_estimate=pl.CostEstimate(flops=flops, bytes_accessed=size, transcendentals=0),
    )(*inputs)


def pairings(peers):
    near = [i ^ 1 for i in range(peers)]
    far = [(i + 1) % peers if i % 2 else (i - 1) % peers for i in range(peers)]
    return near, far


def exchange(near, far):
    to_near, to_far = pairings(lax.axis_size("space"))
    return (
        lax.ppermute(near, "space", list(enumerate(to_near))),
        lax.ppermute(far, "space", list(enumerate(to_far))),
    )


def swapped(value):
    return lax.ppermute(value, "tm", [(0, 1), (1, 0)])


def handed_on(near, far):
    peers = lax.axis_size("space")
    out = []
    for value, to in zip((far, near), pairings(peers)[::-1]):
        perm = [(i, peers + to[i]) for i in range(peers)] + [(peers + i, i) for i in range(peers)]
        out.append(lax.ppermute(value, ("tm", "space"), perm))
    return out


def local(nodes):
    _, _, planes, ny, nz = nodes.shape
    halves, rows, half = nz // LANES, ny // 2, planes // 2
    plane = (halves, 2, rows, LANES)
    field = (planes,) + plane
    quarter = (rows, nz // 2)
    pair = (2,) + quarter
    packed = (3, half) + quarter
    size = planes * ny * nz * 4

    pairs = pair_matrix(nz)
    a_near, a_far = call(
        edge_kernel, "edge_mix", (nodes,), (0,), [plane, plane],
        [
            pltpu.VMEM((2, 3, ny, nz), F32),
            pltpu.VMEM((2, halves, ny, LANES), F32),
            pltpu.SemaphoreType.DMA((2, 3)),
        ],
        limit=EDGE_LIMIT, size=size * 2, flops=size,
    )
    got_a_near, got_a_far = exchange(a_near, a_far)
    one_part, slope, rest, b_near, b_far, coarse_zero, start = call(
        first_kernel, "first_stage", (nodes, pairs), (), [field, field, field, plane, plane, packed, field],
        [pltpu.VMEM((5, ny, LANES), F32), pltpu.VMEM(field, F32)],
        limit=FIRST_LIMIT,
        size=size * 6, flops=size * 10,
    )
    got_b_near, got_b_far = exchange(b_near, b_far)
    one, two_part, coarse_mid, inner, coarse_forces = call(
        second_kernel, "second_stage",
        (one_part, slope, rest, got_a_near, got_a_far, a_near, a_far, pairs, coarse_zero), (),
        [field, (planes + 1,) + plane, packed, (2, 3, halves, rows, LANES), (2, half) + quarter],
        [pltpu.VMEM(field, F32)],
        size=size * 6, flops=size * 10,
    )
    two, h_near, h_far, work = call(
        third_kernel, "third_stage",
        (two_part, got_b_near, got_b_far, inner, coarse_zero, coarse_mid, coarse_forces, pairs), (),
        [(planes + 1,) + plane, pair, pair, (5, half) + quarter], [pltpu.VMEM((2,) + plane, F32)],
        aliases={0: 0}, size=size * 3, flops=size * 5,
    )
    got_near, got_far = exchange(h_near, h_far)
    end, f_near, f_far, swept, two = call(
        fourth_kernel, "coarse_chain", (work, got_near, got_far, h_near, h_far, coarse_forces, two), (6,),
        [(half,) + quarter, pair, pair, (2, half) + quarter, (planes + 1,) + plane],
        any_outs=(4,), aliases={6: 4}, size=size, flops=size,
    )
    ring_far, ring_near = handed_on(f_near, f_far)
    end = swapped(end)
    moved = swapped(two)
    first, change = call(
        step_kernel, "coarse_steps", (ring_far, ring_near, end, work, swept), (),
        [(half,) + quarter, (2, half) + quarter], size=size, flops=size * 50000,
    )
    updated, = call(
        last_kernel, "update",
        (start, first, change, moved, one, two, work), (),
        [(1, 3, planes, ny, nz)],
        [
            pltpu.VMEM((3 * planes, halves, ny, LANES), F32),
            pltpu.VMEM((3 * planes, ny, nz), F32),
            pltpu.SemaphoreType.DMA((3 * planes,)),
        ],
        any_outs=(0,), size=size * 6, flops=size * 5,
    )
    return updated


def solution(mesh):
    in_specs = (P(("groups", "tm"), None, "space", None, None),)
    out_specs = P(("groups", "tm"), None, "space", None, None)
    return jax.shard_map(local, mesh=mesh, in_specs=in_specs, out_specs=out_specs, check_vma=False)
```

```python
import jax
import jax.numpy as jnp
import numpy as np
from jax import lax
from jax.experimental import pallas as pl
from jax.experimental.pallas import tpu as pltpu
from jax.sharding import PartitionSpec as P

DIFFUSE = 0.12
COARSE = DIFFUSE / 4.0
GROWTH = 0.5
WEIGHTS = ((5.0 / 24.0, 1.0 / 3.0, -1.0 / 24.0), (-1.0 / 24.0, 1.0 / 3.0, 5.0 / 24.0))
SECOND = (WEIGHTS[1][0], WEIGHTS[1][1] - 0.5, WEIGHTS[1][2])
LANES = 128
F32 = jnp.float32
BF16 = jnp.bfloat16
VMEM_LIMIT = 32 * 1024 * 1024
EDGE_LIMIT = 52 * 1024 * 1024
FIRST_LIMIT = 48 * 1024 * 1024


def combine(weights, parts):
    return weights[0] * parts[0] + weights[1] * parts[1] + weights[2] * parts[2]


def cube(v):
    return v * v * v


def z_neighbours(halves):
    count = len(halves)
    lane = lax.broadcasted_iota(jnp.int32, halves[0].shape, 1)
    fwd = [pltpu.roll(v, 1, 1) for v in halves]
    back = [pltpu.roll(v, LANES - 1, 1) for v in halves]
    out = []
    for k in range(count):
        before = jnp.where(lane == 0, fwd[(k - 1) % count], fwd[k])
        after = jnp.where(lane == LANES - 1, back[(k + 1) % count], back[k])
        out.append(before + after)
    return out


def y_neighbours(other, parity):
    rows = other.shape[0]
    return other + pltpu.roll(other, 1 if parity == 0 else rows - 1, 0)


def laplace_planes(ref, plane, planes, halves):
    for parity in range(2):
        own = [ref[plane, h, parity] for h in range(halves)]
        side = z_neighbours(own)
        for h in range(halves):
            total = side[h] + y_neighbours(ref[plane, h, 1 - parity], parity) - 6.0 * own[h]
            if plane > 0:
                total = total + ref[plane - 1, h, parity]
            if plane < planes - 1:
                total = total + ref[plane + 1, h, parity]
            yield h, parity, own[h], total


def coarse_force(field):
    planes = len(field)
    out = []
    for p in range(planes):
        v = field[p]
        rows, lanes = v.shape
        total = pltpu.roll(v, 1, 0) + pltpu.roll(v, rows - 1, 0)
        total = total + pltpu.roll(v, 1, 1) + pltpu.roll(v, lanes - 1, 1) - 6.0 * v
        if p > 0:
            total = total + field[p - 1]
        if p < planes - 1:
            total = total + field[p + 1]
        out.append(COARSE * total + GROWTH * (v - cube(v)))
    return out


def split(v):
    high = v.astype(BF16)
    low = (v - high.astype(F32)).astype(BF16)
    return high, low


def pair_matrix(size):
    out = np.zeros((size, size), np.float32)
    for k in range(size // 2):
        for offset in (0, 1):
            out[2 * k + offset, k] = 1.0
            out[2 * k + offset, size // 2 + k] = -1.0
        for offset in (-1, 2):
            out[(2 * k + offset) % size, size // 2 + k] = 1.0
    return jnp.asarray(out, BF16)


def spread_matrix(size):
    row = lax.broadcasted_iota(jnp.int32, (size, 2 * size), 0)
    col = lax.broadcasted_iota(jnp.int32, (size, 2 * size), 1)
    return jnp.where((col == 2 * row) | (col == 2 * row + 1), 1.0, 0.0).astype(F32).astype(BF16)


def times(v, matrix):
    high, low = split(v)
    return jnp.dot(high, matrix, preferred_element_type=F32) + jnp.dot(
        low, matrix, preferred_element_type=F32
    )


def restrict_field(ref, pairs, planes, halves):
    sums, bends = pairs[:, : halves * LANES // 2], pairs[:, halves * LANES // 2 :]

    def y_sum(p):
        return [ref[p, h, 0] + ref[p, h, 1] for h in range(halves)]

    means, forces = [], []
    flat = [y_sum(p) for p in range(planes)]
    for top in range(0, planes, 2):
        total, rest = [], []
        for h in range(halves):
            even = ref[top, h, 0] + ref[top + 1, h, 0]
            odd = ref[top, h, 1] + ref[top + 1, h, 1]
            both = even + odd
            rows = both.shape[0]
            flux = pltpu.roll(odd, 1, 0) + pltpu.roll(even, rows - 1, 0) - 2.0 * both
            if top > 0:
                flux = flux + flat[top - 1][h]
            if top + 2 < planes:
                flux = flux + flat[top + 2][h]
            cubes = cube(ref[top, h, 0]) + cube(ref[top + 1, h, 0])
            cubes = cubes + cube(ref[top, h, 1]) + cube(ref[top + 1, h, 1])
            total.append(both)
            rest.append(DIFFUSE * flux + GROWTH * (both - cubes))
        total = jnp.concatenate(total, axis=1)
        rest = jnp.concatenate(rest, axis=1)
        means.append(times(total, sums) * 0.125)
        forces.append((times(rest, sums) + DIFFUSE * times(total, bends)) * 0.125)
    edges = [times(jnp.concatenate(flat[p], axis=1), sums) for p in (0, planes - 1)]
    return means, forces, edges


def store_coarse(out, means, forces, edges):
    for k, parts in enumerate((means, forces, edges)):
        for p, v in enumerate(parts):
            out[k, p] = v


def outer_planes(planes):
    odd = lax.rem(lax.axis_index("space"), 2)
    return (1 - odd) * (planes - 1), odd * (planes - 1)


def edge_kernel(nodes, near, far, held, work, sem):
    planes, halves = nodes.shape[2], near.shape[0]
    rows = near.shape[2]
    copies = [
        [
            pltpu.make_async_copy(nodes.at[0, m, p], held.at[e, m], sem.at[e, m])
            for m in range(3)
        ]
        for e, p in enumerate(outer_planes(planes))
    ]
    for group in copies:
        for copy in group:
            copy.start()
    for e, out in enumerate((near, far)):
        for copy in copies[e]:
            copy.wait()
        for h in range(halves):
            lanes = pl.ds(h * LANES, LANES)
            work[e, h] = combine(WEIGHTS[0], [held[e, m, :, lanes] for m in range(3)])
            for q in range(2):
                out[h, q] = work[e, h, pl.ds(q, rows, stride=2), :]


def first_kernel(nodes, pairs, one, slope, rest, near, far, coarse, start, work, mix):
    planes, halves = one.shape[0], one.shape[1]
    rows = one.shape[3]
    for p in range(planes):
        for h in range(halves):
            lanes = pl.ds(h * LANES, LANES)
            parts = [nodes[0, m, p, :, lanes] for m in range(3)]
            cubes = [cube(v) for v in parts]
            a = combine(WEIGHTS[0], parts)
            d = combine(SECOND, parts)
            work[0] = parts[0]
            work[1] = a
            work[2] = d
            work[3] = parts[0] + GROWTH * (a - combine(WEIGHTS[0], cubes))
            work[4] = GROWTH * (d - combine(SECOND, cubes))
            for q in range(2):
                for k, out in enumerate((start, mix, slope, one, rest)):
                    out[p, h, q] = work[k, pl.ds(q, rows, stride=2), :]
    for p in range(planes):
        for h, q, _, laplace in laplace_planes(mix, p, planes, halves):
            one[p, h, q] = one[p, h, q] + DIFFUSE * laplace
    for p, out in zip(outer_planes(planes), (near, far)):
        out[...] = 0.5 * one[p] + slope[p]
    store_coarse(coarse, *restrict_field(start, pairs, planes, halves))


def second_kernel(
    one_in, slope, rest, near, far, own_near, own_far, pairs, coarse_zero, one, two, coarse, inner, coarse_forces, mix
):
    planes, halves = one_in.shape[0], one_in.shape[1]
    outer = outer_planes(planes)
    for p in range(1, planes - 1):
        one[p] = one_in[p]
    for p, halo in zip(outer, (near, far)):
        one[p] = one_in[p] + DIFFUSE * halo[...]
    for p in range(planes):
        mix[p] = 0.5 * one[p] + slope[p]
    for p in range(planes):
        for h, q, _, laplace in laplace_planes(mix, p, planes, halves):
            value = one[p, h, q]
            two[p, h, q] = (
                value + DIFFUSE * laplace + (0.5 * GROWTH) * (value - cube(value)) + rest[p, h, q]
            )
    for p, own in zip(outer, (own_near, own_far)):
        two[p] = two[p] + (0.5 * DIFFUSE * DIFFUSE) * own[...]
    for k, p in enumerate((1, planes - 2)):
        for h in range(halves):
            even, odd = two[p, h, 0], two[p, h, 1]
            inner[k, 0, h] = even
            inner[k, 1, h] = odd
            inner[k, 2, h] = GROWTH * (even + odd - cube(even) - cube(odd))
    means, forces, edges = restrict_field(one, pairs, planes, halves)
    store_coarse(coarse, means, forces, edges)
    for k, field in enumerate(([coarse_zero[0, p] for p in range(planes // 2)], means)):
        for p, v in enumerate(coarse_force(field)):
            coarse_forces[k, p] = v


def third_kernel(
    two_in, near, far, inner, coarse_zero, coarse_one, coarse_forces, pairs, two, send_near, send_far, work, outer
):
    planes, halves = two_in.shape[0] - 1, two_in.shape[1]
    later = lax.axis_index("tm").astype(F32)
    for p, halo in zip(outer_planes(planes), (near, far)):
        outer[p // (planes - 1)] = two_in[p] + DIFFUSE * halo[...]
    totals, rests, flats = [], [], []
    other_flats = [[inner[k, 0, h] + inner[k, 1, h] for h in range(halves)] for k in range(2)]
    for k in range(2):
        two[k * (planes - 1)] = outer[k]
        total, rest, flat = [], [], []
        for h in range(halves):
            own = outer[k, h, 0], outer[k, h, 1]
            even, odd = own[0] + inner[k, 0, h], own[1] + inner[k, 1, h]
            line = own[0] + own[1]
            full = line + other_flats[k][h]
            rows = full.shape[0]
            flux = pltpu.roll(odd, 1, 0) + pltpu.roll(even, rows - 1, 0) - 2.0 * full
            flux = flux + other_flats[1 - k][h]
            total.append(full)
            flat.append(line)
            rest.append(
                DIFFUSE * flux + (GROWTH * (line - cube(own[0]) - cube(own[1])) + inner[k, 2, h])
            )
        totals.append(jnp.concatenate(total, axis=1))
        rests.append(jnp.concatenate(rest, axis=1))
        flats.append(jnp.concatenate(flat, axis=1))
    wide = times(jnp.concatenate(totals + flats, axis=0), pairs[...])
    tall = times(jnp.concatenate(rests, axis=0), pairs[:, : halves * LANES // 2])
    rows, lanes = tall.shape[0] // 2, tall.shape[1]
    means_two = [0.125 * wide[k * rows : (k + 1) * rows, :lanes] for k in range(2)]
    edges_two = [wide[k * rows : (k + 1) * rows, :lanes] for k in (2, 3)]
    forces_two = [
        0.125
        * (tall[k * rows : (k + 1) * rows] + DIFFUSE * wide[k * rows : (k + 1) * rows, lanes:])
        for k in range(2)
    ]
    half = planes // 2
    zero = [coarse_zero[0, p] for p in range(half)]
    mean_one = [coarse_one[0, p] for p in range(half)]
    force_zero = [coarse_forces[0, p] for p in range(half)]
    force_one = [coarse_forces[1, p] for p in range(half)]
    sweep_zero, sweep_one = [], []
    for p in range(half):
        parts = (coarse_zero[1, p], coarse_one[1, p], forces_two[p])
        sweep_zero.append(combine(WEIGHTS[0], parts))
        sweep_one.append(combine(WEIGHTS[1], parts))
    sends = []
    for e, p in enumerate((0, half - 1)):
        parts = (coarse_zero[2, e], coarse_one[2, e], edges_two[e])
        partial = sweep_zero[p] - mean_one[p] + (1.0 - later) * zero[p] - (0.5 * later) * force_zero[p]
        sends.append((
            (DIFFUSE / 8.0) * combine(WEIGHTS[0], parts) - (0.5 * COARSE * later) * zero[p],
            (DIFFUSE / 8.0) * combine(WEIGHTS[1], parts) + (0.5 * COARSE) * partial,
        ))
    for k in range(2):
        send_near[k], send_far[k] = low_high(sends[0][k], sends[1][k])
    for p in range(half):
        work[0, p] = zero[p]
        work[1, p] = mean_one[p]
        work[2, p] = means_two[p]
        work[3, p] = sweep_zero[p] - 0.5 * force_zero[p]
        work[4, p] = sweep_one[p] - 0.5 * force_one[p]
        two[planes, 0, p] = means_two[p]


def low_high(near, far):
    odd = lax.rem(lax.axis_index("space"), 2)
    return jnp.where(odd == 1, near, far), jnp.where(odd == 1, far, near)


def sides(near, far):
    pairs = [low_high(near[k], far[k]) for k in range(2)]
    return [v[0] for v in pairs], [v[1] for v in pairs]


def with_halo(work, low, high, own_low, own_high):
    half = work.shape[1]
    one = [work[3, p] for p in range(half)]
    two = [work[4, p] for p in range(half)]
    for p, got, own in ((0, low, own_low), (half - 1, high, own_high)):
        one[p] = one[p] + got[0]
        two[p] = two[p] + got[1] + (0.5 * COARSE) * own[0]
    return one, two


def coarse_steps(first, force, sweep_one, sweep_two):
    half = len(first)
    one = [first[p] + 0.5 * force[p] + sweep_one[p] for p in range(half)]
    force = coarse_force(one)
    return [one[p] + 0.5 * force[p] + sweep_two[p] for p in range(half)]


def fourth_kernel(
    work, near, far, own_near, own_far, coarse_forces, held, end, send_near, send_far, swept, passed
):
    del held, passed
    half = work.shape[1]
    low, high = sides(near, far)
    own_low, own_high = sides(own_near, own_far)
    for k, parts in enumerate(with_halo(work, low, high, own_low, own_high)):
        for p in range(half):
            swept[k, p] = parts[p]

    @pl.when(lax.axis_index("tm") == 0)
    def _():
        first = [work[0, p] for p in range(half)]
        start = [coarse_forces[0, p] for p in range(half)]
        two = coarse_steps(first, start, *[[swept[k, p] for p in range(half)] for k in range(2)])
        force = coarse_force(two)
        for p in range(half):
            end[p] = two[p]
        send_near[0], send_far[0] = low_high(two[0], two[half - 1])
        send_near[1], send_far[1] = low_high(
            two[0] + 0.5 * force[0], two[half - 1] + 0.5 * force[half - 1]
        )


class Planes:
    def __init__(self, updated, parts, result, sem):
        self.updated, self.parts, self.result, self.sem = updated, parts, result, sem
        self.rows = parts.shape[2] // 2
        self.halves = parts.shape[1]
        self.spread = spread_matrix(LANES * self.halves // 2)
        self.copies = []

    def put(self, node, top, change, base):
        wide = times(change, self.spread)
        for p in (2 * top, 2 * top + 1):
            slot = len(self.copies)
            for h in range(self.halves):
                lanes = slice(h * LANES, (h + 1) * LANES)
                for q in range(2):
                    self.parts[slot, h, pl.ds(q, self.rows, stride=2), :] = (
                        base(p, h, q) + wide[:, lanes]
                    )
                self.result[slot, :, lanes] = self.parts[slot, h]
            copy = pltpu.make_async_copy(
                self.result.at[slot], self.updated.at[0, node, p], self.sem.at[slot]
            )
            copy.start()
            self.copies.append(copy)

    def finish(self):
        for copy in self.copies:
            copy.wait()


def arrived_kernel(*refs):
    del refs


def last_kernel(
    own, ring_far, ring_near, end, moved, one, two, work, swept, updated, parts, result, sem
):
    planes, half = one.shape[0], one.shape[0] // 2
    section = lax.axis_index("tm")
    out = Planes(updated, parts, result, sem)
    first = [jnp.where(section == 0, work[0, p], end[p]) for p in range(half)]

    def start(p, h, q):
        return jnp.where(section == 0, own[p, h, q], moved[p, h, q])

    for top in range(half):
        mean = jnp.where(section == 0, work[0, top], moved[planes, 0, top])
        out.put(0, top, first[top] - mean, start)
    ring_low, ring_high = sides(ring_near, ring_far)
    scale = 0.5 * COARSE
    force = coarse_force(first)
    step_one = [first[p] + 0.5 * force[p] + swept[0, p] for p in range(half)]
    for p, v in ((0, ring_low), (half - 1, ring_high)):
        step_one[p] = step_one[p] + jnp.where(section == 0, 0.0, scale * v[0])
    for top in range(half):
        out.put(1, top, step_one[top] - work[1, top], lambda p, h, q: one[p, h, q])
    force = coarse_force(step_one)
    step_two = [step_one[p] + 0.5 * force[p] + swept[1, p] for p in range(half)]
    for p, v in ((0, ring_low), (half - 1, ring_high)):
        step_two[p] = step_two[p] + scale * jnp.where(section == 0, 0.0, v[1] + scale * first[p])
    for top in range(half):
        out.put(2, top, step_two[top] - work[2, top], lambda p, h, q: two[p, h, q])
    out.finish()


def call(kernel, name, inputs, any_inputs, outs, scratch=(), any_outs=(), limit=VMEM_LIMIT,
         aliases=None, flops=0, size=0):
    def spec(far):
        return pl.BlockSpec(memory_space=pl.ANY if far else pltpu.VMEM)

    return pl.pallas_call(
        kernel,
        name=name,
        out_shape=[jax.ShapeDtypeStruct(s, F32) for s in outs],
        in_specs=[spec(k in any_inputs) for k in range(len(inputs))],
        out_specs=[spec(k in any_outs) for k in range(len(outs))],
        scratch_shapes=list(scratch),
        input_output_aliases=aliases or {},
        compiler_params=pltpu.CompilerParams(vmem_limit_bytes=limit),
        cost_estimate=pl.CostEstimate(flops=flops, bytes_accessed=size, transcendentals=0),
    )(*inputs)


def pairings(peers):
    near = [i ^ 1 for i in range(peers)]
    far = [(i + 1) % peers if i % 2 else (i - 1) % peers for i in range(peers)]
    return near, far


def exchange(near, far):
    to_near, to_far = pairings(lax.axis_size("space"))
    return (
        lax.ppermute(near, "space", list(enumerate(to_near))),
        lax.ppermute(far, "space", list(enumerate(to_far))),
    )


def swapped(value):
    return lax.ppermute(value, "tm", [(0, 1), (1, 0)])


def handed_on(near, far):
    peers = lax.axis_size("space")
    out = []
    for value, to in zip((far, near), pairings(peers)[::-1]):
        perm = [(i, peers + to[i]) for i in range(peers)] + [(peers + i, i) for i in range(peers)]
        out.append(lax.ppermute(value, ("tm", "space"), perm))
    return out


def local(nodes):
    _, _, planes, ny, nz = nodes.shape
    halves, rows, half = nz // LANES, ny // 2, planes // 2
    plane = (halves, 2, rows, LANES)
    field = (planes,) + plane
    quarter = (rows, nz // 2)
    pair = (2,) + quarter
    packed = (3, half) + quarter
    size = planes * ny * nz * 4

    pairs = pair_matrix(nz)
    a_near, a_far = call(
        edge_kernel, "edge_mix", (nodes,), (0,), [plane, plane],
        [
            pltpu.VMEM((2, 3, ny, nz), F32),
            pltpu.VMEM((2, halves, ny, LANES), F32),
            pltpu.SemaphoreType.DMA((2, 3)),
        ],
        limit=EDGE_LIMIT, size=size * 2, flops=size,
    )
    got_a_near, got_a_far = exchange(a_near, a_far)
    one_part, slope, rest, b_near, b_far, coarse_zero, start = call(
        first_kernel, "first_stage", (nodes, pairs), (), [field, field, field, plane, plane, packed, field],
        [pltpu.VMEM((5, ny, LANES), F32), pltpu.VMEM(field, F32)],
        limit=FIRST_LIMIT,
        size=size * 6, flops=size * 10,
    )
    got_b_near, got_b_far = exchange(b_near, b_far)
    one, two_part, coarse_mid, inner, coarse_forces = call(
        second_kernel, "second_stage",
        (one_part, slope, rest, got_a_near, got_a_far, a_near, a_far, pairs, coarse_zero), (),
        [field, (planes + 1,) + plane, packed, (2, 3, halves, rows, LANES), (2, half) + quarter],
        [pltpu.VMEM(field, F32)],
        size=size * 6, flops=size * 10,
    )
    two, h_near, h_far, work = call(
        third_kernel, "third_stage",
        (two_part, got_b_near, got_b_far, inner, coarse_zero, coarse_mid, coarse_forces, pairs), (),
        [(planes + 1,) + plane, pair, pair, (5, half) + quarter], [pltpu.VMEM((2,) + plane, F32)],
        aliases={0: 0}, size=size * 3, flops=size * 5,
    )
    got_near, got_far = exchange(h_near, h_far)
    end, f_near, f_far, swept, two = call(
        fourth_kernel, "coarse_chain", (work, got_near, got_far, h_near, h_far, coarse_forces, two), (6,),
        [(half,) + quarter, pair, pair, (2, half) + quarter, (planes + 1,) + plane],
        any_outs=(4,), aliases={6: 4}, size=size, flops=size,
    )
    ring_far, ring_near = handed_on(f_near, f_far)
    end = swapped(end)
    moved = swapped(two)
    ring_far, ring_near, end = call(
        arrived_kernel, "arrived", (ring_far, ring_near, end), (0, 1, 2),
        [pair, pair, (half,) + quarter], any_outs=(0, 1, 2), aliases={0: 0, 1: 1, 2: 2},
        size=size, flops=size * 50000,
    )
    updated, = call(
        last_kernel, "update",
        (start, ring_far, ring_near, end, moved, one, two, work, swept), (),
        [(1, 3, planes, ny, nz)],
        [
            pltpu.VMEM((3 * planes, halves, ny, LANES), F32),
            pltpu.VMEM((3 * planes, ny, nz), F32),
            pltpu.SemaphoreType.DMA((3 * planes,)),
        ],
        any_outs=(0,), size=size * 6, flops=size * 5,
    )
    return updated


def solution(mesh):
    in_specs = (P(("groups", "tm"), None, "space", None, None),)
    out_specs = P(("groups", "tm"), None, "space", None, None)
    return jax.shard_map(local, mesh=mesh, in_specs=in_specs, out_specs=out_specs, check_vma=False)
```

```python
import jax
import jax.numpy as jnp
import numpy as np
from jax import lax
from jax.experimental import pallas as pl
from jax.experimental.pallas import tpu as pltpu
from jax.sharding import PartitionSpec as P

DIFFUSE = 0.12
COARSE = DIFFUSE / 4.0
GROWTH = 0.5
WEIGHTS = ((5.0 / 24.0, 1.0 / 3.0, -1.0 / 24.0), (-1.0 / 24.0, 1.0 / 3.0, 5.0 / 24.0))
SECOND = (WEIGHTS[1][0], WEIGHTS[1][1] - 0.5, WEIGHTS[1][2])
LANES = 128
F32 = jnp.float32
BF16 = jnp.bfloat16
VMEM_LIMIT = 32 * 1024 * 1024
EDGE_LIMIT = 52 * 1024 * 1024
FIRST_LIMIT = 48 * 1024 * 1024


def combine(weights, parts):
    return weights[0] * parts[0] + weights[1] * parts[1] + weights[2] * parts[2]


def cube(v):
    return v * v * v


def z_neighbours(halves):
    count = len(halves)
    lane = lax.broadcasted_iota(jnp.int32, halves[0].shape, 1)
    fwd = [pltpu.roll(v, 1, 1) for v in halves]
    back = [pltpu.roll(v, LANES - 1, 1) for v in halves]
    out = []
    for k in range(count):
        before = jnp.where(lane == 0, fwd[(k - 1) % count], fwd[k])
        after = jnp.where(lane == LANES - 1, back[(k + 1) % count], back[k])
        out.append(before + after)
    return out


def y_neighbours(other, parity):
    rows = other.shape[0]
    return other + pltpu.roll(other, 1 if parity == 0 else rows - 1, 0)


def laplace_planes(ref, plane, planes, halves):
    for parity in range(2):
        own = [ref[plane, h, parity] for h in range(halves)]
        side = z_neighbours(own)
        for h in range(halves):
            total = side[h] + y_neighbours(ref[plane, h, 1 - parity], parity) - 6.0 * own[h]
            if plane > 0:
                total = total + ref[plane - 1, h, parity]
            if plane < planes - 1:
                total = total + ref[plane + 1, h, parity]
            yield h, parity, own[h], total


def coarse_force(field):
    planes = len(field)
    out = []
    for p in range(planes):
        v = field[p]
        rows, lanes = v.shape
        total = pltpu.roll(v, 1, 0) + pltpu.roll(v, rows - 1, 0)
        total = total + pltpu.roll(v, 1, 1) + pltpu.roll(v, lanes - 1, 1) - 6.0 * v
        if p > 0:
            total = total + field[p - 1]
        if p < planes - 1:
            total = total + field[p + 1]
        out.append(COARSE * total + GROWTH * (v - cube(v)))
    return out


def split(v):
    high = v.astype(BF16)
    low = (v - high.astype(F32)).astype(BF16)
    return high, low


def pair_matrix(size):
    out = np.zeros((size, size), np.float32)
    for k in range(size // 2):
        for offset in (0, 1):
            out[2 * k + offset, k] = 1.0
            out[2 * k + offset, size // 2 + k] = -1.0
        for offset in (-1, 2):
            out[(2 * k + offset) % size, size // 2 + k] = 1.0
    return jnp.asarray(out, BF16)


def spread_matrix(size):
    row = lax.broadcasted_iota(jnp.int32, (size, 2 * size), 0)
    col = lax.broadcasted_iota(jnp.int32, (size, 2 * size), 1)
    return jnp.where((col == 2 * row) | (col == 2 * row + 1), 1.0, 0.0).astype(F32).astype(BF16)


def times(v, matrix):
    high, low = split(v)
    return jnp.dot(high, matrix, preferred_element_type=F32) + jnp.dot(
        low, matrix, preferred_element_type=F32
    )


def restrict_field(ref, pairs, planes, halves):
    sums, bends = pairs[:, : halves * LANES // 2], pairs[:, halves * LANES // 2 :]

    def y_sum(p):
        return [ref[p, h, 0] + ref[p, h, 1] for h in range(halves)]

    means, forces = [], []
    flat = [y_sum(p) for p in range(planes)]
    for top in range(0, planes, 2):
        total, rest = [], []
        for h in range(halves):
            even = ref[top, h, 0] + ref[top + 1, h, 0]
            odd = ref[top, h, 1] + ref[top + 1, h, 1]
            both = even + odd
            rows = both.shape[0]
            flux = pltpu.roll(odd, 1, 0) + pltpu.roll(even, rows - 1, 0) - 2.0 * both
            if top > 0:
                flux = flux + flat[top - 1][h]
            if top + 2 < planes:
                flux = flux + flat[top + 2][h]
            cubes = cube(ref[top, h, 0]) + cube(ref[top + 1, h, 0])
            cubes = cubes + cube(ref[top, h, 1]) + cube(ref[top + 1, h, 1])
            total.append(both)
            rest.append(DIFFUSE * flux + GROWTH * (both - cubes))
        total = jnp.concatenate(total, axis=1)
        rest = jnp.concatenate(rest, axis=1)
        means.append(times(total, sums) * 0.125)
        forces.append((times(rest, sums) + DIFFUSE * times(total, bends)) * 0.125)
    edges = [times(jnp.concatenate(flat[p], axis=1), sums) for p in (0, planes - 1)]
    return means, forces, edges


def store_coarse(out, means, forces, edges):
    for k, parts in enumerate((means, forces, edges)):
        for p, v in enumerate(parts):
            out[k, p] = v


def outer_planes(planes):
    odd = lax.rem(lax.axis_index("space"), 2)
    return (1 - odd) * (planes - 1), odd * (planes - 1)


def edge_kernel(nodes, near, far, held, work, sem):
    planes, halves = nodes.shape[2], near.shape[0]
    rows = near.shape[2]
    copies = [
        [
            pltpu.make_async_copy(nodes.at[0, m, p], held.at[e, m], sem.at[e, m])
            for m in range(3)
        ]
        for e, p in enumerate(outer_planes(planes))
    ]
    for group in copies:
        for copy in group:
            copy.start()
    for e, out in enumerate((near, far)):
        for copy in copies[e]:
            copy.wait()
        for h in range(halves):
            lanes = pl.ds(h * LANES, LANES)
            work[e, h] = combine(WEIGHTS[0], [held[e, m, :, lanes] for m in range(3)])
            for q in range(2):
                out[h, q] = work[e, h, pl.ds(q, rows, stride=2), :]


def first_kernel(nodes, pairs, one, slope, rest, near, far, coarse, start, work, mix):
    planes, halves = one.shape[0], one.shape[1]
    rows = one.shape[3]
    for p in range(planes):
        for h in range(halves):
            lanes = pl.ds(h * LANES, LANES)
            parts = [nodes[0, m, p, :, lanes] for m in range(3)]
            cubes = [cube(v) for v in parts]
            a = combine(WEIGHTS[0], parts)
            d = combine(SECOND, parts)
            work[0] = parts[0]
            work[1] = a
            work[2] = d
            work[3] = parts[0] + GROWTH * (a - combine(WEIGHTS[0], cubes))
            work[4] = GROWTH * (d - combine(SECOND, cubes))
            for q in range(2):
                for k, out in enumerate((start, mix, slope, one, rest)):
                    out[p, h, q] = work[k, pl.ds(q, rows, stride=2), :]
    for p in range(planes):
        for h, q, _, laplace in laplace_planes(mix, p, planes, halves):
            one[p, h, q] = one[p, h, q] + DIFFUSE * laplace
    for p, out in zip(outer_planes(planes), (near, far)):
        out[...] = 0.5 * one[p] + slope[p]
    store_coarse(coarse, *restrict_field(start, pairs, planes, halves))


def second_kernel(
    one_in, slope, rest, near, far, own_near, own_far, pairs, coarse_zero, one, two, coarse, inner, coarse_forces, mix
):
    planes, halves = one_in.shape[0], one_in.shape[1]
    outer = outer_planes(planes)
    for p in range(1, planes - 1):
        one[p] = one_in[p]
    for p, halo in zip(outer, (near, far)):
        one[p] = one_in[p] + DIFFUSE * halo[...]
    for p in range(planes):
        mix[p] = 0.5 * one[p] + slope[p]
    for p in range(planes):
        for h, q, _, laplace in laplace_planes(mix, p, planes, halves):
            value = one[p, h, q]
            two[p, h, q] = (
                value + DIFFUSE * laplace + (0.5 * GROWTH) * (value - cube(value)) + rest[p, h, q]
            )
    for p, own in zip(outer, (own_near, own_far)):
        two[p] = two[p] + (0.5 * DIFFUSE * DIFFUSE) * own[...]
    for k, p in enumerate((1, planes - 2)):
        for h in range(halves):
            even, odd = two[p, h, 0], two[p, h, 1]
            inner[k, 0, h] = even
            inner[k, 1, h] = odd
            inner[k, 2, h] = GROWTH * (even + odd - cube(even) - cube(odd))
    means, forces, edges = restrict_field(one, pairs, planes, halves)
    store_coarse(coarse, means, forces, edges)
    for k, field in enumerate(([coarse_zero[0, p] for p in range(planes // 2)], means)):
        for p, v in enumerate(coarse_force(field)):
            coarse_forces[k, p] = v


def third_kernel(
    two_in, near, far, inner, coarse_zero, coarse_one, coarse_forces, pairs, two, send_near, send_far, work, outer
):
    planes, halves = two_in.shape[0] - 1, two_in.shape[1]
    later = lax.axis_index("tm").astype(F32)
    for p, halo in zip(outer_planes(planes), (near, far)):
        outer[p // (planes - 1)] = two_in[p] + DIFFUSE * halo[...]
    totals, rests, flats = [], [], []
    other_flats = [[inner[k, 0, h] + inner[k, 1, h] for h in range(halves)] for k in range(2)]
    for k in range(2):
        two[k * (planes - 1)] = outer[k]
        total, rest, flat = [], [], []
        for h in range(halves):
            own = outer[k, h, 0], outer[k, h, 1]
            even, odd = own[0] + inner[k, 0, h], own[1] + inner[k, 1, h]
            line = own[0] + own[1]
            full = line + other_flats[k][h]
            rows = full.shape[0]
            flux = pltpu.roll(odd, 1, 0) + pltpu.roll(even, rows - 1, 0) - 2.0 * full
            flux = flux + other_flats[1 - k][h]
            total.append(full)
            flat.append(line)
            rest.append(
                DIFFUSE * flux + (GROWTH * (line - cube(own[0]) - cube(own[1])) + inner[k, 2, h])
            )
        totals.append(jnp.concatenate(total, axis=1))
        rests.append(jnp.concatenate(rest, axis=1))
        flats.append(jnp.concatenate(flat, axis=1))
    wide = times(jnp.concatenate(totals + flats, axis=0), pairs[...])
    tall = times(jnp.concatenate(rests, axis=0), pairs[:, : halves * LANES // 2])
    rows, lanes = tall.shape[0] // 2, tall.shape[1]
    means_two = [0.125 * wide[k * rows : (k + 1) * rows, :lanes] for k in range(2)]
    edges_two = [wide[k * rows : (k + 1) * rows, :lanes] for k in (2, 3)]
    forces_two = [
        0.125
        * (tall[k * rows : (k + 1) * rows] + DIFFUSE * wide[k * rows : (k + 1) * rows, lanes:])
        for k in range(2)
    ]
    half = planes // 2
    zero = [coarse_zero[0, p] for p in range(half)]
    mean_one = [coarse_one[0, p] for p in range(half)]
    force_zero = [coarse_forces[0, p] for p in range(half)]
    force_one = [coarse_forces[1, p] for p in range(half)]
    sweep_zero, sweep_one = [], []
    for p in range(half):
        parts = (coarse_zero[1, p], coarse_one[1, p], forces_two[p])
        sweep_zero.append(combine(WEIGHTS[0], parts))
        sweep_one.append(combine(WEIGHTS[1], parts))
    sends = []
    for e, p in enumerate((0, half - 1)):
        parts = (coarse_zero[2, e], coarse_one[2, e], edges_two[e])
        partial = sweep_zero[p] - mean_one[p] + (1.0 - later) * zero[p] - (0.5 * later) * force_zero[p]
        sends.append((
            (DIFFUSE / 8.0) * combine(WEIGHTS[0], parts) - (0.5 * COARSE * later) * zero[p],
            (DIFFUSE / 8.0) * combine(WEIGHTS[1], parts) + (0.5 * COARSE) * partial,
        ))
    for k in range(2):
        send_near[k], send_far[k] = low_high(sends[0][k], sends[1][k])
    for p in range(half):
        work[0, p] = zero[p]
        work[1, p] = mean_one[p]
        work[2, p] = means_two[p]
        work[3, p] = sweep_zero[p] - 0.5 * force_zero[p]
        work[4, p] = sweep_one[p] - 0.5 * force_one[p]
        two[planes, 0, p] = means_two[p]


def low_high(near, far):
    odd = lax.rem(lax.axis_index("space"), 2)
    return jnp.where(odd == 1, near, far), jnp.where(odd == 1, far, near)


def sides(near, far):
    pairs = [low_high(near[k], far[k]) for k in range(2)]
    return [v[0] for v in pairs], [v[1] for v in pairs]


def with_halo(work, low, high, own_low, own_high):
    half = work.shape[1]
    one = [work[3, p] for p in range(half)]
    two = [work[4, p] for p in range(half)]
    for p, got, own in ((0, low, own_low), (half - 1, high, own_high)):
        one[p] = one[p] + got[0]
        two[p] = two[p] + got[1] + (0.5 * COARSE) * own[0]
    return one, two


def coarse_steps(first, force, sweep_one, sweep_two):
    half = len(first)
    one = [first[p] + 0.5 * force[p] + sweep_one[p] for p in range(half)]
    force = coarse_force(one)
    return [one[p] + 0.5 * force[p] + sweep_two[p] for p in range(half)]


def fourth_kernel(
    work, near, far, own_near, own_far, coarse_forces, held, end, send_near, send_far, swept, passed
):
    del held, passed
    half = work.shape[1]
    low, high = sides(near, far)
    own_low, own_high = sides(own_near, own_far)
    for k, parts in enumerate(with_halo(work, low, high, own_low, own_high)):
        for p in range(half):
            swept[k, p] = parts[p]

    @pl.when(lax.axis_index("tm") == 0)
    def _():
        first = [work[0, p] for p in range(half)]
        start = [coarse_forces[0, p] for p in range(half)]
        two = coarse_steps(first, start, *[[swept[k, p] for p in range(half)] for k in range(2)])
        force = coarse_force(two)
        for p in range(half):
            end[p] = two[p]
        send_near[0], send_far[0] = low_high(two[0], two[half - 1])
        send_near[1], send_far[1] = low_high(
            two[0] + 0.5 * force[0], two[half - 1] + 0.5 * force[half - 1]
        )


class Planes:
    def __init__(self, updated, parts, result, sem):
        self.updated, self.parts, self.result, self.sem = updated, parts, result, sem
        self.rows = parts.shape[2] // 2
        self.halves = parts.shape[1]
        self.spread = spread_matrix(LANES * self.halves // 2)
        self.copies = []

    def put(self, node, top, change, base):
        wide = times(change, self.spread)
        for p in (2 * top, 2 * top + 1):
            slot = len(self.copies)
            for h in range(self.halves):
                lanes = slice(h * LANES, (h + 1) * LANES)
                for q in range(2):
                    self.parts[slot, h, pl.ds(q, self.rows, stride=2), :] = (
                        base(p, h, q) + wide[:, lanes]
                    )
                self.result[slot, :, lanes] = self.parts[slot, h]
            copy = pltpu.make_async_copy(
                self.result.at[slot], self.updated.at[0, node, p], self.sem.at[slot]
            )
            copy.start()
            self.copies.append(copy)

    def finish(self):
        for copy in self.copies:
            copy.wait()


def step_kernel(ring_far, ring_near, end, work, swept, first, change):
    half = work.shape[1]
    section = lax.axis_index("tm")
    ring_low, ring_high = sides(ring_near, ring_far)
    scale = 0.5 * COARSE
    start = [jnp.where(section == 0, work[0, p], end[p]) for p in range(half)]
    force = coarse_force(start)
    one = [start[p] + 0.5 * force[p] + swept[0, p] for p in range(half)]
    for p, v in ((0, ring_low), (half - 1, ring_high)):
        one[p] = one[p] + jnp.where(section == 0, 0.0, scale * v[0])
    force = coarse_force(one)
    two = [one[p] + 0.5 * force[p] + swept[1, p] for p in range(half)]
    for p, v in ((0, ring_low), (half - 1, ring_high)):
        two[p] = two[p] + scale * jnp.where(section == 0, 0.0, v[1] + scale * start[p])
    for p in range(half):
        first[p] = start[p]
        change[0, p] = one[p] - work[1, p]
        change[1, p] = two[p] - work[2, p]


def last_kernel(
    own, first, change, moved, one, two, work, updated, parts, result, sem
):
    planes, half = one.shape[0], one.shape[0] // 2
    section = lax.axis_index("tm")
    out = Planes(updated, parts, result, sem)
    def start(p, h, q):
        return jnp.where(section == 0, own[p, h, q], moved[p, h, q])

    for top in range(half):
        mean = jnp.where(section == 0, work[0, top], moved[planes, 0, top])
        out.put(0, top, first[top] - mean, start)
    for top in range(half):
        out.put(1, top, change[0, top], lambda p, h, q: one[p, h, q])
    for top in range(half):
        out.put(2, top, change[1, top], lambda p, h, q: two[p, h, q])
    out.finish()


def call(kernel, name, inputs, any_inputs, outs, scratch=(), any_outs=(), limit=VMEM_LIMIT,
         aliases=None, flops=0, size=0):
    def spec(far):
        return pl.BlockSpec(memory_space=pl.ANY if far else pltpu.VMEM)

    return pl.pallas_call(
        kernel,
        name=name,
        out_shape=[jax.ShapeDtypeStruct(s, F32) for s in outs],
        in_specs=[spec(k in any_inputs) for k in range(len(inputs))],
        out_specs=[spec(k in any_outs) for k in range(len(outs))],
        scratch_shapes=list(scratch),
        input_output_aliases=aliases or {},
        compiler_params=pltpu.CompilerParams(vmem_limit_bytes=limit),
        cost_estimate=pl.CostEstimate(flops=flops, bytes_accessed=size, transcendentals=0),
    )(*inputs)


def pairings(peers):
    near = [i ^ 1 for i in range(peers)]
    far = [(i + 1) % peers if i % 2 else (i - 1) % peers for i in range(peers)]
    return near, far


def exchange(near, far):
    to_near, to_far = pairings(lax.axis_size("space"))
    return (
        lax.ppermute(near, "space", list(enumerate(to_near))),
        lax.ppermute(far, "space", list(enumerate(to_far))),
    )


def swapped(value):
    return lax.ppermute(value, "tm", [(0, 1), (1, 0)])


def handed_on(near, far):
    peers = lax.axis_size("space")
    out = []
    for value, to in zip((far, near), pairings(peers)[::-1]):
        perm = [(i, peers + to[i]) for i in range(peers)] + [(peers + i, i) for i in range(peers)]
        out.append(lax.ppermute(value, ("tm", "space"), perm))
    return out


def local(nodes):
    _, _, planes, ny, nz = nodes.shape
    halves, rows, half = nz // LANES, ny // 2, planes // 2
    plane = (halves, 2, rows, LANES)
    field = (planes,) + plane
    quarter = (rows, nz // 2)
    pair = (2,) + quarter
    packed = (3, half) + quarter
    size = planes * ny * nz * 4

    pairs = pair_matrix(nz)
    a_near, a_far = call(
        edge_kernel, "edge_mix", (nodes,), (0,), [plane, plane],
        [
            pltpu.VMEM((2, 3, ny, nz), F32),
            pltpu.VMEM((2, halves, ny, LANES), F32),
            pltpu.SemaphoreType.DMA((2, 3)),
        ],
        limit=EDGE_LIMIT, size=size * 2, flops=size,
    )
    got_a_near, got_a_far = exchange(a_near, a_far)
    one_part, slope, rest, b_near, b_far, coarse_zero, start = call(
        first_kernel, "first_stage", (nodes, pairs), (), [field, field, field, plane, plane, packed, field],
        [pltpu.VMEM((5, ny, LANES), F32), pltpu.VMEM(field, F32)],
        limit=FIRST_LIMIT,
        size=size * 6, flops=size * 10,
    )
    got_b_near, got_b_far = exchange(b_near, b_far)
    one, two_part, coarse_mid, inner, coarse_forces = call(
        second_kernel, "second_stage",
        (one_part, slope, rest, got_a_near, got_a_far, a_near, a_far, pairs, coarse_zero), (),
        [field, (planes + 1,) + plane, packed, (2, 3, halves, rows, LANES), (2, half) + quarter],
        [pltpu.VMEM(field, F32)],
        size=size * 6, flops=size * 10,
    )
    two, h_near, h_far, work = call(
        third_kernel, "third_stage",
        (two_part, got_b_near, got_b_far, inner, coarse_zero, coarse_mid, coarse_forces, pairs), (),
        [(planes + 1,) + plane, pair, pair, (5, half) + quarter], [pltpu.VMEM((2,) + plane, F32)],
        aliases={0: 0}, size=size * 3, flops=size * 5,
    )
    got_near, got_far = exchange(h_near, h_far)
    end, f_near, f_far, swept, two = call(
        fourth_kernel, "coarse_chain", (work, got_near, got_far, h_near, h_far, coarse_forces, two), (6,),
        [(half,) + quarter, pair, pair, (2, half) + quarter, (planes + 1,) + plane],
        any_outs=(4,), aliases={6: 4}, size=size, flops=size,
    )
    ring_far, ring_near = handed_on(f_near, f_far)
    end = swapped(end)
    moved = swapped(two)
    first, change = call(
        step_kernel, "coarse_steps", (ring_far, ring_near, end, work, swept), (),
        [(half,) + quarter, (2, half) + quarter], size=size, flops=size * 50000,
    )
    updated, = call(
        last_kernel, "update",
        (start, first, change, moved, one, two, work), (),
        [(1, 3, planes, ny, nz)],
        [
            pltpu.VMEM((3 * planes, halves, ny, LANES), F32),
            pltpu.VMEM((3 * planes, ny, nz), F32),
            pltpu.SemaphoreType.DMA((3 * planes,)),
        ],
        any_outs=(0,), size=size * 6, flops=size * 5,
    )
    return updated


def solution(mesh):
    in_specs = (P(("groups", "tm"), None, "space", None, None),)
    out_specs = P(("groups", "tm"), None, "space", None, None)
    return jax.shard_map(local, mesh=mesh, in_specs=in_specs, out_specs=out_specs, check_vma=False)
```
